32 devices in a mesh: ctx: 8 (over y, x, core), head: 4 (over z).
Axes of the slice: x: 2, y: 2, z: 4, core: 2. Of those that a mesh axis runs over, the one named last changes fastest.
Arguments:
- attn_q: bfloat16 [4096, 2048], P(('ctx', 'head')), may hold values from -6 to 6
- attn_k: bfloat16 [4096, 2048], P(('ctx', 'head')), may hold values from -6 to 6
- attn_v: bfloat16 [4096, 2048], P(('ctx', 'head')), may hold values from -6 to 6
- step_size: float32 [4, 4096], P('head', 'ctx'), may hold values from 0.05 to 1
- fast_init: float32 [4, 3, 512, 512], P('head'), may hold values from -0.25 to 0.25
- boundary: int32 [1], replicated, may hold values from 1024 to 3071
- window_len: int32 [16], replicated, may hold values from 2 to 128, as said below
Outputs:
- layer_out: bfloat16 [4096, 2048], P('ctx', 'head')
The draws below stay inside these ranges and needn't reach their ends.
Inputs may be any that keep to these rules, and one draw needn't show every extreme that they name: `window_len`: some attention head has a window of exactly 128.
All inputs are finite; a program needn't handle non-finite values.
Results may differ from the reference program's by a relative error of at most 0.017.
Values may be sent and summed in bfloat16 or wider, within the bound.
A program may use at most 64 MiB of HBM per device.

```python
import math
import jax
import jax.numpy as jnp
from jax import lax

D = 2048
FW = 512
AH = 128
WIN = 128
NS_STEPS = 2
NA = 16
FH = 4
TOKENS = 4096


def query_key_pair(key):
    base_q = jax.random.truncated_normal(jax.random.fold_in(key, 11), -6.0, 6.0, (TOKENS, D), jnp.float32)
    base_k = jax.random.truncated_normal(jax.random.fold_in(key, 12), -6.0, 6.0, (TOKENS, D), jnp.float32)
    return (base_q, base_k)


def draw_attn_q(key, part):
    return query_key_pair(key)[0].astype(jnp.bfloat16)


def draw_attn_k(key, part):
    return query_key_pair(key)[1].astype(jnp.bfloat16)


def draw_window_len(key, part):
    lengths = jax.random.randint(jax.random.fold_in(key, 21), (NA,), 2, WIN + 1, dtype=jnp.int32)
    widest = jax.random.randint(jax.random.fold_in(key, 22), (), 0, NA, dtype=jnp.int32)
    return jnp.where(jnp.arange(NA, dtype=jnp.int32) == widest, WIN, lengths).astype(jnp.int32)


def block_scale(key, extent, cuts, low, high):
    def one(dim, shards_of):
        heights = jax.random.uniform(jax.random.fold_in(jax.random.fold_in(key, 6), dim), (shards_of,), jnp.float32, low / len(cuts), high / len(cuts))
        return jnp.repeat(jnp.exp(heights), extent[dim] // shards_of).reshape((-1,) + (1,) * (len(extent) - dim - 1))

    gain = one(*cuts[0])
    for cut in cuts[1:]:
        gain = gain * one(*cut)
    return gain


def normal_values(rng, dims, scale, bound, cuts=(), kind=jnp.bfloat16):
    drawn = jax.random.normal(rng, dims, jnp.float32) * scale
    if len(cuts) > 0:
        drawn = block_scale(rng, dims, cuts, -0.22, 0.18) * drawn
    return jnp.clip(drawn, min=-bound, max=bound).astype(kind)


def setup_inputs(seed: int = 0) -> dict:
    splits = jax.random.split(jax.random.key(seed), 8)
    return {
        "attn_q": draw_attn_q(jax.random.fold_in(splits[7], 71), 0),
        "attn_k": draw_attn_k(jax.random.fold_in(splits[7], 71), 0),
        "attn_v": normal_values(splits[2], (TOKENS, D), 1.0, 6.0, ((0, 32),)),
        "step_size": jnp.clip(jnp.exp(math.log(1.0) - 2.9957323 * jax.random.uniform(splits[3], (FH, TOKENS), jnp.float32) ** block_scale(splits[3], (FH, TOKENS), ((0, 4), (1, 8)), -0.2, 0.2)), 0.05, 1.0),
        "fast_init": normal_values(splits[4], (FH, 3, FW, FW), FW ** -0.5, 0.25, ((0, 4),), jnp.float32),
        "boundary": jax.random.randint(splits[5], (1,), TOKENS // 4, 3 * TOKENS // 4).astype(jnp.int32),
        "window_len": draw_window_len(jax.random.fold_in(splits[7], 71), 0),
    }


ns_linear = 3.4445
ns_cubic = -4.775
ns_quintic = 2.0315

def rms_norm(values):
    x_wide = values.astype(jnp.float32)
    return x_wide / jnp.sqrt(lax.optimization_barrier(jnp.mean(x_wide * x_wide, axis=-1, keepdims=True)) + 1e-06)

def attend_rows(scores, q_pos, k_pos, window_len, v_blk):
    pos_gap = q_pos[:, None] - k_pos[None, :]
    allowed = (pos_gap[None] >= 0) & (pos_gap[None] < window_len[:, None, None]) & (k_pos[None, None, :] >= 0)
    masked = jnp.where(allowed, scores, -jnp.inf)
    row_peak = lax.optimization_barrier(jnp.max(masked, axis=-1, keepdims=True))
    expo_val = jnp.exp(masked - row_peak)
    weights_bf = (expo_val / lax.optimization_barrier(jnp.sum(expo_val, axis=-1, keepdims=True))).astype(jnp.bfloat16)
    mixed = jnp.einsum('hqk,khd->qhd', weights_bf.astype(jnp.float32), v_blk)
    return mixed.astype(jnp.bfloat16)

def window_attention(queries, key_rows, value_rows, window_len):
    zero_pad = jnp.zeros((WIN, D), jnp.bfloat16)
    keys_pad = jnp.concatenate([zero_pad, key_rows], axis=0)
    values_pad = jnp.concatenate([zero_pad, value_rows], axis=0)

    def one_block(block_id):
        row_start = block_id * WIN
        q_blk = lax.dynamic_slice_in_dim(queries, row_start, WIN, 0).reshape(WIN, NA, AH).astype(jnp.float32)
        k_blk = lax.dynamic_slice_in_dim(keys_pad, row_start, 2 * WIN, 0).reshape(2 * WIN, NA, AH).astype(jnp.float32)
        v_blk = lax.dynamic_slice_in_dim(values_pad, row_start, 2 * WIN, 0).reshape(2 * WIN, NA, AH).astype(jnp.float32)
        scores = jnp.einsum('qhd,khd->hqk', q_blk, k_blk) / math.sqrt(AH)
        q_pos = row_start + jnp.arange(WIN, dtype=jnp.int32)
        k_pos = row_start - WIN + jnp.arange(2 * WIN, dtype=jnp.int32)
        return attend_rows(scores, q_pos, k_pos, window_len, v_blk).reshape(WIN, D)
    blocks = lax.map(one_block, jnp.arange(TOKENS // WIN, dtype=jnp.int32))
    return blocks.reshape(TOKENS, D)

def swiglu_grads(fast_k, fast_v, token_scale, weights):
    w_bf = weights.astype(jnp.bfloat16)
    pre_gate = jnp.dot(fast_k, w_bf[0], preferred_element_type=jnp.float32)
    pre_up = jnp.dot(fast_k, w_bf[1], preferred_element_type=jnp.float32)
    gate_sig = jax.nn.sigmoid(pre_gate)
    gate_act = pre_gate * gate_sig
    hidden = (gate_act * pre_up).astype(jnp.bfloat16)
    target = (fast_v.astype(jnp.float32) * token_scale[:, None]).astype(jnp.bfloat16)
    grad_down = jnp.dot(hidden.T, target, preferred_element_type=jnp.float32)
    back_out = jnp.dot(target, w_bf[2].T, preferred_element_type=jnp.float32)
    back_gate = (back_out * pre_up * gate_sig * (1.0 + pre_gate * (1.0 - gate_sig))).astype(jnp.bfloat16)
    back_up = (back_out * gate_act).astype(jnp.bfloat16)
    grad_gate = jnp.dot(fast_k.T, back_gate, preferred_element_type=jnp.float32)
    grad_up = jnp.dot(fast_k.T, back_up, preferred_element_type=jnp.float32)
    return jnp.stack([grad_gate, grad_up, grad_down])

def swiglu_apply(fast_q, weights):
    w_bf = weights.astype(jnp.bfloat16)
    pre_gate = jnp.dot(fast_q, w_bf[0], preferred_element_type=jnp.float32)
    pre_up = jnp.dot(fast_q, w_bf[1], preferred_element_type=jnp.float32)
    hidden = (pre_gate * jax.nn.sigmoid(pre_gate) * pre_up).astype(jnp.bfloat16)
    return jnp.dot(hidden, w_bf[2], preferred_element_type=jnp.float32)

def newton_schulz(grad_sum):
    norm_sq = lax.optimization_barrier(jnp.sum(grad_sum * grad_sum, axis=(1, 2)))
    ortho_bf = (grad_sum / (jnp.sqrt(norm_sq) + 1e-07)[:, None, None]).astype(jnp.bfloat16)
    for ns_step in range(NS_STEPS):
        x_wide = ortho_bf.astype(jnp.float32)
        square = jnp.einsum('bij,bkj->bik', x_wide, x_wide).astype(jnp.bfloat16)
        square_wide = square.astype(jnp.float32)
        quartic = jnp.einsum('bij,bjk->bik', square_wide, square_wide)
        mixer_bf = (ns_cubic * square_wide + ns_quintic * quartic).astype(jnp.bfloat16)
        ortho_bf = (ns_linear * x_wide + jnp.einsum('bij,bjk->bik', mixer_bf.astype(jnp.float32), x_wide)).astype(jnp.bfloat16)
    return ortho_bf

def reference(attn_q, attn_k, attn_v, step_size, fast_init, boundary, window_len):
    attended = window_attention(attn_q, attn_k, attn_v, window_len)
    in_first = jnp.arange(TOKENS, dtype=jnp.int32) < boundary[0]
    outputs = []
    for head_id in range(FH):
        col_lo = head_id * FW
        fast_q = rms_norm(attn_q[:, col_lo:col_lo + FW]).astype(jnp.bfloat16)
        fast_k = rms_norm(attn_k[:, col_lo:col_lo + FW]).astype(jnp.bfloat16)
        fast_v = attn_v[:, col_lo:col_lo + FW]
        weights = fast_init[head_id]
        result = jnp.zeros((TOKENS, FW), jnp.float32)
        for section_id in range(2):
            inside = in_first if section_id == 0 else jnp.logical_not(in_first)
            token_scale = step_size[head_id] * inside.astype(jnp.float32)
            grad_sum = swiglu_grads(fast_k, fast_v, token_scale, weights)
            weights = weights + newton_schulz(grad_sum).astype(jnp.float32)
            result = jnp.where(inside[:, None], swiglu_apply(fast_q, weights), result)
        combined = attended[:, col_lo:col_lo + FW].astype(jnp.float32) + rms_norm(result)
        outputs.append(combined.astype(jnp.bfloat16))
    return jnp.concatenate(outputs, axis=1)
```

```python
import functools
import math

import jax
import jax.numpy as jnp
from jax import lax
from jax.experimental import pallas as pl
from jax.experimental.pallas import tpu as pltpu
from jax.sharding import PartitionSpec as P

AH = 128
WIN = 128
NS_STEPS = 2
LAG = 2
ns_linear = 3.4445
ns_cubic = -4.775
ns_quintic = 2.0315
MESH = pl.DeviceIdType.MESH
F32 = jnp.float32
BF = jnp.bfloat16


def sum_plan(rows, n_bits):
    half = rows // 2
    quarter = half // 2
    offset = half
    transfers = 1
    groups = []
    for order in (list(range(1, n_bits)), list(range(n_bits - 1, 0, -1))):
        size = quarter
        steps = []
        for bit in order:
            halve = size // 2 >= 16
            sent = size // 2 if halve else size
            steps.append((bit, halve, size, sent, offset, transfers))
            offset += sent
            transfers += 1
            size = sent
        groups.append((steps, size))
    back = transfers
    transfers += 2 * (n_bits - 1) + 1
    return groups, offset, back, transfers


def kernel(
    n_ctx, n_head, q_hbm, k_hbm, v_hbm, step_ref, init_hbm, bound_ref, win_ref, out_ref,
    q_all, k_all, v_all, kb, qb, step_t, w32, wb, pre_g, pre_u, back, hid, tgt, bg, bu, xs, sq, mx,
    grad, attended, res1, sb, rb, red,
    loc_sem, a2a_send, a2a_recv, halo_send, halo_recv, ar_send, ar_recv,
):
    ctx = lax.axis_index("ctx")
    head = lax.axis_index("head")
    n_bits = n_ctx.bit_length() - 1
    tok = q_hbm.shape[0]
    fw = q_all.shape[1]
    count = q_all.shape[0]
    half = fw // 2
    quarter = half // 2
    groups, _, back_at, _ = sum_plan(fw, n_bits)

    def bit_of(b):
        return lax.rem(lax.div(ctx, 1 << b), 2)

    def partner(b):
        return ctx + (1 << b) - 2 * (1 << b) * bit_of(b)

    nxt = lax.rem(ctx + 1, n_ctx)
    prv = lax.rem(ctx + n_ctx - 1, n_ctx)

    barrier = pltpu.get_barrier_semaphore()
    for d in range(1, n_head):
        pl.semaphore_signal(
            barrier, inc=1, device_id={"head": lax.rem(head + d, n_head)}, device_id_type=MESH
        )
    for b in range(n_bits):
        pl.semaphore_signal(barrier, inc=1, device_id={"ctx": partner(b)}, device_id_type=MESH)
    pl.semaphore_signal(barrier, inc=1, device_id={"ctx": nxt}, device_id_type=MESH)
    pl.semaphore_signal(barrier, inc=1, device_id={"ctx": prv}, device_id_type=MESH)

    my_cols = pl.ds(pl.multiple_of(head * fw, fw), fw)

    def own_copy(i, src, dst, first):
        rows = pl.ds(pl.multiple_of(first + head * tok, tok), tok)
        return pltpu.make_async_copy(src.at[:, my_cols], dst.at[rows, :], loc_sem.at[i])

    locals_ = [own_copy(0, k_hbm, k_all, WIN), own_copy(1, v_hbm, v_all, WIN), own_copy(2, q_hbm, q_all, 0)]
    init_copy = pltpu.make_async_copy(init_hbm.at[0], w32, loc_sem.at[3])
    for c in locals_:
        c.start()
    init_copy.start()

    pl.semaphore_wait(barrier, n_head - 1 + n_bits + 2)

    def spread(i, src, dst, first):
        copies = []
        for d in range(1, n_head):
            to = lax.rem(head + d, n_head)
            cols = pl.ds(pl.multiple_of(to * fw, fw), fw)
            rows = pl.ds(pl.multiple_of(first + head * tok, tok), tok)
            copies.append(
                pltpu.make_async_remote_copy(
                    src_ref=src.at[:, cols],
                    dst_ref=dst.at[rows, :],
                    send_sem=a2a_send.at[i, d - 1],
                    recv_sem=a2a_recv.at[i, d - 1],
                    device_id={"head": to},
                    device_id_type=MESH,
                )
            )
        return copies

    k_copies = spread(0, k_hbm, k_all, WIN)
    v_copies = spread(1, v_hbm, v_all, WIN)
    q_copies = spread(2, q_hbm, q_all, 0)
    for c in k_copies + v_copies:
        c.start()
    sent = k_copies + v_copies + q_copies

    for i in range(count // 128):
        wide = jnp.broadcast_to(step_ref[0:1, i * 128 : (i + 1) * 128], (128, 128))
        step_t[i * 128 : (i + 1) * 128, :] = wide.T

    init_copy.wait()
    for m in range(3):
        wb[m] = w32[m].astype(BF)

    def chunks(rows, body, size=64):
        def go(i, carry):
            body(pl.ds(pl.multiple_of(i * size, size), size), i * size)
            return carry

        lax.fori_loop(0, rows // size, go, 0)

    def rms(x):
        return x * lax.rsqrt(jnp.mean(x * x, axis=-1, keepdims=True) + 1e-06)

    def dot(a, b, ca=1, cb=0):
        return lax.dot_general(a, b, (((ca,), (cb,)), ((), ())), preferred_element_type=F32)

    def rms_keys(rows, first):
        kb[rows, :] = rms(k_all[pl.ds(pl.multiple_of(first + WIN, 64), 64), :].astype(F32)).astype(BF)

    def rms_queries(rows, first):
        qb[rows, :] = rms(q_all[rows, :].astype(F32)).astype(BF)

    def inside(first, size, block):
        pos = ctx * count + first + lax.broadcasted_iota(jnp.int32, (size, 128), 0)
        early = pos < bound_ref[0]
        return early if block == 0 else jnp.logical_not(early)

    def make_target(block):
        def body(rows, first):
            col = jnp.where(inside(first, 64, block), step_t[rows, :], 0.0)
            scale = jnp.concatenate([col] * (fw // 128), axis=1)
            v = v_all[pl.ds(pl.multiple_of(first + WIN, 64), 64), :].astype(F32)
            tgt[rows, :] = (v * scale).astype(BF)

        chunks(count, body)

    def make_hidden():
        def body(rows, first):
            g = pre_g[rows, :]
            u = pre_u[rows, :]
            act = g * jax.nn.sigmoid(g)
            hid[rows, :] = (act * u).astype(BF)

        chunks(count, body)

    def make_back():
        def body(rows, first):
            g = pre_g[rows, :]
            u = pre_u[rows, :]
            o = back[rows, :]
            sig = jax.nn.sigmoid(g)
            bg[rows, :] = (o * u * sig * (1.0 + g * (1.0 - sig))).astype(BF)
            bu[rows, :] = (o * (g * sig)).astype(BF)

        chunks(count, body)

    def ctx_copy(block, m, src, dst, t, bit):
        c = pltpu.make_async_remote_copy(
            src_ref=src,
            dst_ref=dst,
            send_sem=ar_send.at[block, m, t],
            recv_sem=ar_recv.at[block, m, t],
            device_id={"ctx": partner(bit)},
            device_id_type=MESH,
        )
        c.start()
        sent.append(c)
        return c

    def al(x, n):
        return pl.multiple_of(x, n)

    def sum_steps(block, m):
        mine = bit_of(0) * half
        other = half - mine
        state = {}

        def first():
            sb[block, m, 0:half, :] = grad[m, pl.ds(al(other, half), half), :].astype(BF)
            state["c"] = [
                ctx_copy(block, m, sb.at[block, m, pl.ds(0, half)], rb.at[block, m, pl.ds(0, half)], 0, 0)
            ]
            state["base"] = [mine, mine + quarter]

        def land_first():
            state["c"][0].wait_recv()
            rows = pl.ds(al(mine, half), half)
            grad[m, rows, :] = grad[m, rows, :] + rb[block, m, 0:half, :].astype(F32)

        def launch(s):
            state["c"] = []
            for g, (steps, _) in enumerate(groups):
                bit, halve, size, part, off, t = steps[s]
                base = state["base"][g]
                if halve:
                    src = base + (1 - bit_of(bit)) * part
                    state["base"][g] = base + bit_of(bit) * part
                else:
                    src = base
                sb[block, m, off : off + part, :] = grad[m, pl.ds(al(src, part), part), :].astype(BF)
                area = pl.ds(off, part)
                state["c"].append(
                    ctx_copy(block, m, sb.at[block, m, area], rb.at[block, m, area], t, bit)
                )

        def land(s):
            for g, (steps, _) in enumerate(groups):
                bit, halve, size, part, off, t = steps[s]
                state["c"][g].wait_recv()
                rows = pl.ds(al(state["base"][g], part), part)
                grad[m, rows, :] = grad[m, rows, :] + rb[block, m, off : off + part, :].astype(F32)

        def settle():
            for g, (_, size) in enumerate(groups):
                rows = pl.ds(al(state["base"][g], size), size)
                red[block, m, rows, :] = grad[m, rows, :].astype(BF)

        n_steps = n_bits - 1

        def return_launch(s):
            state["c"] = []
            for g, (steps, _) in enumerate(groups):
                bit, halve, size, part, off, t = steps[s]
                if not halve:
                    continue
                rows = pl.ds(al(state["base"][g], part), part)
                here = red.at[block, m, rows]
                state["c"].append(
                    ctx_copy(block, m, here, here, back_at + g * n_steps + s, bit)
                )

        def return_land(s):
            for c in state["c"]:
                c.wait_recv()
            for g, (steps, _) in enumerate(groups):
                bit, halve, size, part, off, t = steps[s]
                if halve:
                    state["base"][g] = state["base"][g] - bit_of(bit) * part

        def last_launch():
            here = red.at[block, m, pl.ds(al(mine, half), half)]
            state["c"] = [ctx_copy(block, m, here, here, back_at + 2 * n_steps, 0)]

        def last_land():
            state["c"][0].wait_recv()

        acts = [first, land_first]
        for s in range(n_steps):
            acts += [functools.partial(launch, s), functools.partial(land, s)]
        acts.append(settle)
        for s in reversed(range(n_steps)):
            acts += [functools.partial(return_launch, s), functools.partial(return_land, s)]
        acts += [last_launch, last_land]
        steps, now = [], []
        for a in acts:
            name = a.func if isinstance(a, functools.partial) else a
            now.append(a)
            if name in (first, launch, return_launch, last_launch):
                steps.append(now)
                now = []
        steps.append(now)
        return steps

    def newton_schulz(block, m):
        r = red[block, m].astype(F32)
        inv = 1.0 / (jnp.sqrt(jnp.sum(r * r, keepdims=True)) + 1e-07)
        xs[...] = (r * inv).astype(BF)
        for _ in range(NS_STEPS):
            sq[...] = dot(xs[...], xs[...], 1, 1).astype(BF)
            mx[...] = (ns_cubic * sq[...].astype(F32) + ns_quintic * dot(sq[...], sq[...])).astype(BF)
            xs[...] = (ns_linear * xs[...].astype(F32) + dot(mx[...], xs[...])).astype(BF)
        new = w32[m] + xs[...].astype(F32)
        w32[m] = new
        wb[m] = new.astype(BF)

    ORDER = (2, 0, 1)

    def run_sums(block, before, after, fillers):
        todo = []
        for i, m in enumerate(ORDER):
            for s, acts in enumerate(sum_steps(block, m)):
                todo.append((s + LAG * i if s > 0 else 0, i, s, m, acts))
            n_steps = s
        todo.sort(key=lambda x: (x[0], x[1]))
        fillers = list(fillers)
        level = 0
        for at, i, s, m, acts in todo:
            if at != level:
                level = at
                if fillers and level > 1:
                    fillers.pop(0)()
            if s == 0:
                before[m]()
            for a in acts:
                a()
            if s == n_steps:
                after[m]()
        for f in fillers:
            f()

    def attend(j):
        cols = slice(j * AH, (j + 1) * AH)
        reach = win_ref[head * (fw // AH) + j]
        for i in range(count // WIN):
            q = q_all[i * WIN : (i + 1) * WIN, cols]
            keys = k_all[i * WIN : (i + 2) * WIN, cols]
            vals = v_all[i * WIN : (i + 2) * WIN, cols]
            scores = dot(q, keys, 1, 1) * (1.0 / math.sqrt(AH))
            row = lax.broadcasted_iota(jnp.int32, (WIN, 2 * WIN), 0)
            col = lax.broadcasted_iota(jnp.int32, (WIN, 2 * WIN), 1)
            gap = row + WIN - col
            allowed = (gap >= 0) & (gap < reach)
            if i == 0:
                allowed = allowed & (ctx * count - WIN + col >= 0)
            masked = jnp.where(allowed, scores, -jnp.inf)
            e = jnp.exp(masked - jnp.max(masked, axis=-1, keepdims=True))
            w = (e * (1.0 / jnp.sum(e, axis=-1, keepdims=True))).astype(BF)
            attended[i * WIN : (i + 1) * WIN, cols] = dot(w, vals).astype(BF)

    def apply_hidden():
        pre_g[...] = dot(qb[...], wb[0])
        pre_u[...] = dot(qb[...], wb[1])
        make_hidden()

    for c in locals_[:1]:
        c.wait()
    for c in k_copies:
        c.wait_recv()
    chunks(count, rms_keys)
    pre_g[...] = dot(kb[...], wb[0])
    pre_u[...] = dot(kb[...], wb[1])
    make_hidden()
    locals_[1].wait()
    for c in v_copies:
        c.wait_recv()
    for c in q_copies:
        c.start()
    halos = []
    for i, ref in enumerate((k_all, v_all)):
        c = pltpu.make_async_remote_copy(
            src_ref=ref.at[pl.ds(count, WIN)],
            dst_ref=ref.at[pl.ds(0, WIN)],
            send_sem=halo_send.at[i],
            recv_sem=halo_recv.at[i],
            device_id={"ctx": nxt},
            device_id_type=MESH,
        )
        c.start()
        halos.append(c)
        sent.append(c)

    def grad_down():
        grad[2] = dot(hid[...], tgt[...], 0, 0)

    def grad_gate():
        back[...] = dot(tgt[...], wb[2], 1, 1)
        make_back()
        grad[0] = dot(kb[...], bg[...], 0, 0)

    def grad_up():
        grad[1] = dot(kb[...], bu[...], 0, 0)

    before = {2: grad_down, 0: grad_gate, 1: grad_up}

    def after_for(block):
        return {m: functools.partial(newton_schulz, block, m) for m in range(3)}

    def got_queries():
        locals_[2].wait()
        for c in q_copies:
            c.wait_recv()
        chunks(count, rms_queries)
        for c in halos:
            c.wait_recv()

    make_target(0)
    run_sums(0, before, after_for(0), [])
    pre_g[...] = dot(kb[...], wb[0])
    pre_u[...] = dot(kb[...], wb[1])
    make_hidden()
    make_target(1)

    def finish_rows(rows, first):
        early = jnp.concatenate([inside(first, 64, 0)] * (fw // 128), axis=1)
        r = rms(jnp.where(early, res1[rows, :], back[rows, :]))
        out_ref[rows, :] = (attended[rows, :].astype(F32) + r).astype(BF)

    def early_out():
        apply_hidden()
        res1[...] = dot(hid[...], wb[2])

    fill = [got_queries, early_out] + [functools.partial(attend, j) for j in range(fw // AH)]
    run_sums(1, before, after_for(1), fill)
    apply_hidden()
    back[...] = dot(hid[...], wb[2])
    chunks(count, finish_rows)
    for c in sent:
        c.wait_send()


def local(attn_q, attn_k, attn_v, step_size, fast_init, boundary, window_len):
    n_ctx = lax.axis_size("ctx")
    n_head = lax.axis_size("head")
    tok, width = attn_q.shape
    fw = width // n_head
    count = tok * n_head
    _, staged, _, transfers = sum_plan(fw, n_ctx.bit_length() - 1)
    hbm = pl.BlockSpec(memory_space=pl.ANY)
    vmem = pl.BlockSpec(memory_space=pltpu.VMEM)
    smem = pl.BlockSpec(memory_space=pltpu.SMEM)
    big = lambda dtype, *lead: pltpu.VMEM(lead + (count, fw), dtype)
    mat = lambda dtype, *lead: pltpu.VMEM(lead + (fw, fw), dtype)
    return pl.pallas_call(
        functools.partial(kernel, n_ctx, n_head),
        out_shape=jax.ShapeDtypeStruct((count, fw), BF),
        in_specs=[hbm, hbm, hbm, vmem, hbm, smem, smem],
        out_specs=vmem,
        scratch_shapes=[
            big(BF),
            pltpu.VMEM((count + WIN, fw), BF),
            pltpu.VMEM((count + WIN, fw), BF),
            big(BF),
            big(BF),
            pltpu.VMEM((count, 128), F32),
            mat(F32, 3),
            mat(BF, 3),
            big(F32),
            big(F32),
            big(F32),
            big(BF),
            big(BF),
            big(BF),
            big(BF),
            mat(BF),
            mat(BF),
            mat(BF),
            mat(F32, 3),
            big(BF),
            big(F32),
            pltpu.VMEM((2, 3, staged, fw), BF),
            pltpu.VMEM((2, 3, staged, fw), BF),
            mat(BF, 2, 3),
            pltpu.SemaphoreType.DMA((4,)),
            pltpu.SemaphoreType.DMA((3, n_head - 1)),
            pltpu.SemaphoreType.DMA((3, n_head - 1)),
            pltpu.SemaphoreType.DMA((2,)),
            pltpu.SemaphoreType.DMA((2,)),
            pltpu.SemaphoreType.DMA((2, 3, transfers)),
            pltpu.SemaphoreType.DMA((2, 3, transfers)),
        ],
        compiler_params=pltpu.CompilerParams(
            collective_id=0, has_side_effects=True, vmem_limit_bytes=48 * 1024 * 1024
        ),
    )(attn_q, attn_k, attn_v, step_size, fast_init, boundary, window_len)


def solution(mesh):
    return jax.shard_map(
        local,
        mesh=mesh,
        in_specs=(
            P(("ctx", "head"), None),
            P(("ctx", "head"), None),
            P(("ctx", "head"), None),
            P("head", "ctx"),
            P("head", None, None, None),
            P(),
            P(),
        ),
        out_specs=P("ctx", "head"),
        check_vma=False,
    )
```

```python
import functools
import math

import jax
import jax.numpy as jnp
from jax import lax
from jax.experimental import pallas as pl
from jax.experimental.pallas import tpu as pltpu
from jax.sharding import PartitionSpec as P

AH = 128
WIN = 128
NS_STEPS = 2
LAG = 1
ns_linear = 3.4445
ns_cubic = -4.775
ns_quintic = 2.0315
MESH = pl.DeviceIdType.MESH
F32 = jnp.float32
BF = jnp.bfloat16


def sum_plan(rows, n_bits):
    half = rows // 2
    quarter = half // 2
    offset = half
    transfers = 1
    groups = []
    for order in (list(range(1, n_bits)), list(range(n_bits - 1, 0, -1))):
        size = quarter
        steps = []
        for bit in order:
            halve = size // 2 >= 16
            sent = size // 2 if halve else size
            steps.append((bit, halve, size, sent, offset, transfers))
            offset += sent
            transfers += 1
            size = sent
        groups.append((steps, size))
    back = transfers
    transfers += 2 * (n_bits - 1) + 1
    return groups, offset, back, transfers


def kernel(
    n_ctx, n_head, q_hbm, k_hbm, v_hbm, step_ref, init_hbm, bound_ref, win_ref, out_ref,
    q_all, k_all, v_all, kb, kbt, qb, step_t, w32, wb, pre_g, pre_u, back, hid, tgt, bg, bu, xs, sq, mx,
    grad, attended, res1, sb, rb, red,
    loc_sem, a2a_send, a2a_recv, halo_send, halo_recv, ar_send, ar_recv,
):
    ctx = lax.axis_index("ctx")
    head = lax.axis_index("head")
    n_bits = n_ctx.bit_length() - 1
    tok = q_hbm.shape[0]
    fw = q_all.shape[1]
    count = q_all.shape[0]
    half = fw // 2
    quarter = half // 2
    groups, _, back_at, _ = sum_plan(fw, n_bits)

    def bit_of(b):
        return lax.rem(lax.div(ctx, 1 << b), 2)

    def partner(b):
        return ctx + (1 << b) - 2 * (1 << b) * bit_of(b)

    nxt = lax.rem(ctx + 1, n_ctx)
    prv = lax.rem(ctx + n_ctx - 1, n_ctx)

    barrier = pltpu.get_barrier_semaphore()
    for d in range(1, n_head):
        pl.semaphore_signal(
            barrier, inc=1, device_id={"head": lax.rem(head + d, n_head)}, device_id_type=MESH
        )
    for b in range(n_bits):
        pl.semaphore_signal(barrier, inc=1, device_id={"ctx": partner(b)}, device_id_type=MESH)
    pl.semaphore_signal(barrier, inc=1, device_id={"ctx": nxt}, device_id_type=MESH)
    pl.semaphore_signal(barrier, inc=1, device_id={"ctx": prv}, device_id_type=MESH)

    my_cols = pl.ds(pl.multiple_of(head * fw, fw), fw)

    def own_copy(i, src, dst, first):
        rows = pl.ds(pl.multiple_of(first + head * tok, tok), tok)
        return pltpu.make_async_copy(src.at[:, my_cols], dst.at[rows, :], loc_sem.at[i])

    locals_ = [own_copy(0, k_hbm, k_all, WIN), own_copy(1, v_hbm, v_all, WIN), own_copy(2, q_hbm, q_all, 0)]
    init_copy = pltpu.make_async_copy(init_hbm.at[0], w32, loc_sem.at[3])
    for c in locals_:
        c.start()
    init_copy.start()

    pl.semaphore_wait(barrier, n_head - 1 + n_bits + 2)

    def spread(i, src, dst, first):
        copies = []
        for d in range(1, n_head):
            to = lax.rem(head + d, n_head)
            cols = pl.ds(pl.multiple_of(to * fw, fw), fw)
            rows = pl.ds(pl.multiple_of(first + head * tok, tok), tok)
            copies.append(
                pltpu.make_async_remote_copy(
                    src_ref=src.at[:, cols],
                    dst_ref=dst.at[rows, :],
                    send_sem=a2a_send.at[i, d - 1],
                    recv_sem=a2a_recv.at[i, d - 1],
                    device_id={"head": to},
                    device_id_type=MESH,
                )
            )
        return copies

    k_copies = spread(0, k_hbm, k_all, WIN)
    v_copies = spread(1, v_hbm, v_all, WIN)
    q_copies = spread(2, q_hbm, q_all, 0)
    for c in k_copies + v_copies:
        c.start()
    sent = k_copies + v_copies + q_copies

    for i in range(count // 128):
        wide = jnp.broadcast_to(step_ref[0:1, i * 128 : (i + 1) * 128], (128, 128))
        step_t[i * 128 : (i + 1) * 128, :] = wide.T

    init_copy.wait()
    for m in range(3):
        wb[m] = w32[m].astype(BF)

    def chunks(rows, body, size=64):
        def go(i, carry):
            body(pl.ds(pl.multiple_of(i * size, size), size), i * size)
            return carry

        lax.fori_loop(0, rows // size, go, 0)

    def rms(x):
        return x * lax.rsqrt(jnp.mean(x * x, axis=-1, keepdims=True) + 1e-06)

    def dot(a, b, ca=1, cb=0):
        return lax.dot_general(a, b, (((ca,), (cb,)), ((), ())), preferred_element_type=F32)

    def rms_keys(rows, first):
        kb[rows, :] = rms(k_all[pl.ds(pl.multiple_of(first + WIN, 64), 64), :].astype(F32)).astype(BF)

    def rms_queries(rows, first):
        qb[rows, :] = rms(q_all[rows, :].astype(F32)).astype(BF)

    def inside(first, size, block):
        pos = ctx * count + first + lax.broadcasted_iota(jnp.int32, (size, 128), 0)
        early = pos < bound_ref[0]
        return early if block == 0 else jnp.logical_not(early)

    def make_target(block):
        def body(rows, first):
            col = jnp.where(inside(first, 64, block), step_t[rows, :], 0.0)
            scale = jnp.concatenate([col] * (fw // 128), axis=1)
            v = v_all[pl.ds(pl.multiple_of(first + WIN, 64), 64), :].astype(F32)
            tgt[rows, :] = (v * scale).astype(BF)

        chunks(count, body)

    def make_hidden():
        def body(rows, first):
            g = pre_g[rows, :]
            u = pre_u[rows, :]
            act = g * jax.nn.sigmoid(g)
            hid[rows, :] = (act * u).astype(BF)

        chunks(count, body)

    def make_back(with_hidden):
        def body(rows, first):
            g = pre_g[rows, :]
            u = pre_u[rows, :]
            o = back[rows, :]
            sig = jax.nn.sigmoid(g)
            act = g * sig
            if with_hidden:
                hid[rows, :] = (act * u).astype(BF)
            bg[rows, :] = (o * u * sig * (1.0 + g * (1.0 - sig))).astype(BF)
            bu[rows, :] = (o * act).astype(BF)

        chunks(count, body)

    def ctx_copy(block, m, src, dst, t, bit):
        c = pltpu.make_async_remote_copy(
            src_ref=src,
            dst_ref=dst,
            send_sem=ar_send.at[block, m, t],
            recv_sem=ar_recv.at[block, m, t],
            device_id={"ctx": partner(bit)},
            device_id_type=MESH,
        )
        c.start()
        sent.append(c)
        return c

    def al(x, n):
        return pl.multiple_of(x, n)

    def sum_steps(block, m):
        mine = bit_of(0) * half
        other = half - mine
        state = {}

        def first():
            sb[block, m, 0:half, :] = grad[m, pl.ds(al(other, half), half), :].astype(BF)
            state["c"] = [
                ctx_copy(block, m, sb.at[block, m, pl.ds(0, half)], rb.at[block, m, pl.ds(0, half)], 0, 0)
            ]
            state["base"] = [mine, mine + quarter]

        def land_first():
            state["c"][0].wait_recv()
            rows = pl.ds(al(mine, half), half)
            grad[m, rows, :] = grad[m, rows, :] + rb[block, m, 0:half, :].astype(F32)

        def launch(s):
            state["c"] = []
            for g, (steps, _) in enumerate(groups):
                bit, halve, size, part, off, t = steps[s]
                base = state["base"][g]
                if halve:
                    src = base + (1 - bit_of(bit)) * part
                    state["base"][g] = base + bit_of(bit) * part
                else:
                    src = base
                sb[block, m, off : off + part, :] = grad[m, pl.ds(al(src, part), part), :].astype(BF)
                area = pl.ds(off, part)
                state["c"].append(
                    ctx_copy(block, m, sb.at[block, m, area], rb.at[block, m, area], t, bit)
                )

        def land(s):
            for g, (steps, _) in enumerate(groups):
                bit, halve, size, part, off, t = steps[s]
                state["c"][g].wait_recv()
                rows = pl.ds(al(state["base"][g], part), part)
                grad[m, rows, :] = grad[m, rows, :] + rb[block, m, off : off + part, :].astype(F32)

        def settle():
            for g, (_, size) in enumerate(groups):
                rows = pl.ds(al(state["base"][g], size), size)
                red[block, m, rows, :] = grad[m, rows, :].astype(BF)

        n_steps = n_bits - 1

        def return_launch(s):
            state["c"] = []
            for g, (steps, _) in enumerate(groups):
                bit, halve, size, part, off, t = steps[s]
                if not halve:
                    continue
                rows = pl.ds(al(state["base"][g], part), part)
                here = red.at[block, m, rows]
                state["c"].append(
                    ctx_copy(block, m, here, here, back_at + g * n_steps + s, bit)
                )

        def return_land(s):
            for c in state["c"]:
                c.wait_recv()
            for g, (steps, _) in enumerate(groups):
                bit, halve, size, part, off, t = steps[s]
                if halve:
                    state["base"][g] = state["base"][g] - bit_of(bit) * part

        def last_launch():
            here = red.at[block, m, pl.ds(al(mine, half), half)]
            state["c"] = [ctx_copy(block, m, here, here, back_at + 2 * n_steps, 0)]

        def last_land():
            state["c"][0].wait_recv()

        acts = [first, land_first]
        for s in range(n_steps):
            acts += [functools.partial(launch, s), functools.partial(land, s)]
        acts.append(settle)
        for s in reversed(range(n_steps)):
            acts += [functools.partial(return_launch, s), functools.partial(return_land, s)]
        acts += [last_launch, last_land]
        steps, now = [], []
        for a in acts:
            name = a.func if isinstance(a, functools.partial) else a
            now.append(a)
            if name in (first, launch, return_launch, last_launch):
                steps.append(now)
                now = []
        steps.append(now)
        return steps

    def newton_schulz(block, m):
        r = red[block, m].astype(F32)
        inv = 1.0 / (jnp.sqrt(jnp.sum(r * r, keepdims=True)) + 1e-07)
        xs[...] = (r * inv).astype(BF)
        for _ in range(NS_STEPS):
            sq[...] = dot(xs[...], xs[...], 1, 1).astype(BF)
            mx[...] = (ns_cubic * sq[...].astype(F32) + ns_quintic * dot(sq[...], sq[...])).astype(BF)
            xs[...] = (ns_linear * xs[...].astype(F32) + dot(mx[...], xs[...])).astype(BF)
        new = w32[m] + xs[...].astype(F32)
        w32[m] = new
        wb[m] = new.astype(BF)

    ORDER = (2, 0, 1)

    def run_sums(block, before, after, fillers):
        todo = []
        for i, m in enumerate(ORDER):
            for s, acts in enumerate(sum_steps(block, m)):
                todo.append((s + LAG * i if s > 0 else 0, i, s, m, acts))
            n_steps = s
        fillers = list(fillers)
        for level in range(n_steps + LAG * (len(ORDER) - 1) + 1):
            work = []
            for at, i, s, m, acts in todo:
                if at != level:
                    continue
                if s == 0:
                    before[m]()
                for a in acts:
                    a()
                if s == n_steps:
                    work.append(after[m])
            if level > 0 and fillers:
                fillers.pop(0)()
            for w in work:
                w()
        for f in fillers:
            f()

    def attend(j):
        cols = slice(j * AH, (j + 1) * AH)
        reach = win_ref[head * (fw // AH) + j]
        for i in range(count // WIN):
            q = q_all[i * WIN : (i + 1) * WIN, cols]
            keys = k_all[i * WIN : (i + 2) * WIN, cols]
            vals = v_all[i * WIN : (i + 2) * WIN, cols]
            scores = dot(q, keys, 1, 1) * (1.0 / math.sqrt(AH))
            row = lax.broadcasted_iota(jnp.int32, (WIN, 2 * WIN), 0)
            col = lax.broadcasted_iota(jnp.int32, (WIN, 2 * WIN), 1)
            gap = row + WIN - col
            allowed = (gap >= 0) & (gap < reach)
            if i == 0:
                allowed = allowed & (ctx * count - WIN + col >= 0)
            masked = jnp.where(allowed, scores, -jnp.inf)
            e = jnp.exp(masked - jnp.max(masked, axis=-1, keepdims=True))
            w = (e * (1.0 / jnp.sum(e, axis=-1, keepdims=True))).astype(BF)
            attended[i * WIN : (i + 1) * WIN, cols] = dot(w, vals).astype(BF)

    for c in locals_[:1]:
        c.wait()
    for c in k_copies:
        c.wait_recv()
    chunks(count, rms_keys)
    kbt[...] = kb[...].T
    pre_g[...] = dot(kb[...], wb[0])
    pre_u[...] = dot(kb[...], wb[1])
    make_hidden()
    locals_[1].wait()
    for c in v_copies:
        c.wait_recv()
    for c in q_copies:
        c.start()
    halos = []
    for i, ref in enumerate((k_all, v_all)):
        halos.append(
            pltpu.make_async_remote_copy(
                src_ref=ref.at[pl.ds(count, WIN)],
                dst_ref=ref.at[pl.ds(0, WIN)],
                send_sem=halo_send.at[i],
                recv_sem=halo_recv.at[i],
                device_id={"ctx": nxt},
                device_id_type=MESH,
            )
        )
    sent.extend(halos)

    def grad_down():
        grad[2] = dot(hid[...], tgt[...], 0, 0)

    def grad_gate():
        grad[0] = dot(kbt[...], bg[...])

    def grad_up():
        grad[1] = dot(kbt[...], bu[...])

    def first_gate():
        back[...] = dot(tgt[...], wb[2], 1, 1)
        make_back(False)
        grad_gate()

    def mid_down():
        newton_schulz(0, 2)
        make_target(1)
        back[...] = dot(tgt[...], wb[2], 1, 1)

    def mid_gate():
        newton_schulz(0, 0)
        pre_g[...] = dot(kb[...], wb[0])

    def mid_up():
        for c in halos:
            c.start()
        newton_schulz(0, 1)
        pre_u[...] = dot(kb[...], wb[1])
        make_back(True)

    def end_down():
        newton_schulz(1, 2)

    def end_gate():
        newton_schulz(1, 0)
        pre_g[...] = dot(qb[...], wb[0])

    def end_up():
        newton_schulz(1, 1)
        pre_u[...] = dot(qb[...], wb[1])

    def got_queries():
        locals_[2].wait()
        for c in q_copies:
            c.wait_recv()
        chunks(count, rms_queries)
        pre_g[...] = dot(qb[...], wb[0])
        pre_u[...] = dot(qb[...], wb[1])

    def early_out():
        make_hidden()
        res1[...] = dot(hid[...], wb[2])

    def attend_first():
        for c in halos:
            c.wait_recv()
        attend(0)

    def finish_rows(rows, first):
        early = jnp.concatenate([inside(first, 64, 0)] * (fw // 128), axis=1)
        r = rms(jnp.where(early, res1[rows, :], back[rows, :]))
        out_ref[rows, :] = (attended[rows, :].astype(F32) + r).astype(BF)

    make_target(0)
    run_sums(0, {2: grad_down, 0: first_gate, 1: grad_up}, {2: mid_down, 0: mid_gate, 1: mid_up}, [])
    fill = [got_queries, early_out, attend_first]
    fill += [functools.partial(attend, j) for j in range(1, fw // AH)]
    run_sums(
        1, {2: grad_down, 0: grad_gate, 1: grad_up}, {2: end_down, 0: end_gate, 1: end_up}, fill
    )
    make_hidden()
    back[...] = dot(hid[...], wb[2])
    chunks(count, finish_rows)
    for c in sent:
        c.wait_send()


def local(attn_q, attn_k, attn_v, step_size, fast_init, boundary, window_len):
    n_ctx = lax.axis_size("ctx")
    n_head = lax.axis_size("head")
    tok, width = attn_q.shape
    fw = width // n_head
    count = tok * n_head
    _, staged, _, transfers = sum_plan(fw, n_ctx.bit_length() - 1)
    hbm = pl.BlockSpec(memory_space=pltpu.HBM)
    vmem = pl.BlockSpec(memory_space=pltpu.VMEM)
    smem = pl.BlockSpec(memory_space=pltpu.SMEM)
    big = lambda dtype, *lead: pltpu.VMEM(lead + (count, fw), dtype)
    mat = lambda dtype, *lead: pltpu.VMEM(lead + (fw, fw), dtype)
    return pl.pallas_call(
        functools.partial(kernel, n_ctx, n_head),
        out_shape=jax.ShapeDtypeStruct((count, fw), BF),
        in_specs=[hbm, hbm, hbm, vmem, hbm, smem, smem],
        out_specs=vmem,
        scratch_shapes=[
            big(BF),
            pltpu.VMEM((count + WIN, fw), BF),
            pltpu.VMEM((count + WIN, fw), BF),
            big(BF),
            pltpu.VMEM((fw, count), BF),
            big(BF),
            pltpu.VMEM((count, 128), F32),
            mat(F32, 3),
            mat(BF, 3),
            big(F32),
            big(F32),
            big(F32),
            big(BF),
            big(BF),
            big(BF),
            big(BF),
            mat(BF),
            mat(BF),
            mat(BF),
            mat(F32, 3),
            big(BF),
            big(F32),
            pltpu.VMEM((2, 3, staged, fw), BF),
            pltpu.VMEM((2, 3, staged, fw), BF),
            mat(BF, 2, 3),
            pltpu.SemaphoreType.DMA((4,)),
            pltpu.SemaphoreType.DMA((3, n_head - 1)),
            pltpu.SemaphoreType.DMA((3, n_head - 1)),
            pltpu.SemaphoreType.DMA((2,)),
            pltpu.SemaphoreType.DMA((2,)),
            pltpu.SemaphoreType.DMA((2, 3, transfers)),
            pltpu.SemaphoreType.DMA((2, 3, transfers)),
        ],
        compiler_params=pltpu.CompilerParams(
            collective_id=0, has_side_effects=True, vmem_limit_bytes=60 * 1024 * 1024
        ),
    )(attn_q, attn_k, attn_v, step_size, fast_init, boundary, window_len)


def solution(mesh):
    return jax.shard_map(
        local,
        mesh=mesh,
        in_specs=(
            P(("ctx", "head"), None),
            P(("ctx", "head"), None),
            P(("ctx", "head"), None),
            P("head", "ctx"),
            P("head", None, None, None),
            P(),
            P(),
        ),
        out_specs=P("ctx", "head"),
        check_vma=False,
    )
```

```python
import functools
import math

import jax
import jax.numpy as jnp
from jax import lax
from jax.experimental import pallas as pl
from jax.experimental.pallas import tpu as pltpu
from jax.sharding import PartitionSpec as P

AH = 128
WIN = 128
NS_STEPS = 2
LAG = 1
ns_linear = 3.4445
ns_cubic = -4.775
ns_quintic = 2.0315
MESH = pl.DeviceIdType.MESH
F32 = jnp.float32
BF = jnp.bfloat16


def sum_plan(rows, n_bits):
    half = rows // 2
    quarter = half // 2
    offset = half
    transfers = 1
    groups = []
    for order in (list(range(1, n_bits)), list(range(n_bits - 1, 0, -1))):
        size = quarter
        steps = []
        for bit in order:
            halve = size // 2 >= 16
            sent = size // 2 if halve else size
            steps.append((bit, halve, size, sent, offset, transfers))
            offset += sent
            transfers += 1
            size = sent
        groups.append((steps, size))
    back = transfers
    transfers += 2 * (n_bits - 1) + 1
    return groups, offset, back, transfers


def kernel(
    n_ctx, n_head, q_hbm, k_hbm, v_hbm, step_hbm, init_hbm, bound_hbm, win_hbm, out_ref,
    q_all, k_all, v_all, kb, kbt, qb, step_t, w32, wb, pre, back, hid, tgt, bg, bu, xs, sq, mx,
    grad, attended, res1, sb, rb, red, x_out, x_in, step_ref, bound_ref, win_ref,
    loc_sem, a2a_send, a2a_recv, halo_send, halo_recv, ar_send, ar_recv, x_send, x_recv,
):
    ctx = lax.axis_index("ctx")
    head = lax.axis_index("head")
    n_bits = n_ctx.bit_length() - 1
    tok = q_hbm.shape[0]
    fw = q_all.shape[1]
    count = q_all.shape[0]
    half = fw // 2
    quarter = half // 2
    groups, _, back_at, _ = sum_plan(fw, n_bits)

    def bit_of(b):
        return lax.rem(lax.div(ctx, 1 << b), 2)

    def partner(b):
        return ctx + (1 << b) - 2 * (1 << b) * bit_of(b)

    nxt = lax.rem(ctx + 1, n_ctx)
    prv = lax.rem(ctx + n_ctx - 1, n_ctx)

    barrier = pltpu.get_barrier_semaphore()
    for d in range(1, n_head):
        pl.semaphore_signal(
            barrier, inc=1, device_id={"head": lax.rem(head + d, n_head)}, device_id_type=MESH
        )
    for b in range(n_bits):
        pl.semaphore_signal(barrier, inc=1, device_id={"ctx": partner(b)}, device_id_type=MESH)
    pl.semaphore_signal(barrier, inc=1, device_id={"ctx": nxt}, device_id_type=MESH)
    pl.semaphore_signal(barrier, inc=1, device_id={"ctx": prv}, device_id_type=MESH)

    my_cols = pl.ds(pl.multiple_of(head * fw, fw), fw)

    def own_copy(i, src, dst, first):
        rows = pl.ds(pl.multiple_of(first + head * tok, tok), tok)
        return pltpu.make_async_copy(src.at[:, my_cols], dst.at[rows, :], loc_sem.at[i])

    locals_ = [own_copy(0, k_hbm, k_all, WIN), own_copy(1, v_hbm, v_all, WIN), own_copy(2, q_hbm, q_all, 0)]
    init_copy = pltpu.make_async_copy(init_hbm.at[0], w32, loc_sem.at[3])
    for c in locals_:
        c.start()
    init_copy.start()
    small = [
        pltpu.make_async_copy(src, dst, loc_sem.at[4 + i])
        for i, (src, dst) in enumerate(
            ((step_hbm, step_ref), (bound_hbm, bound_ref), (win_hbm, win_ref))
        )
    ]
    for c in small:
        c.start()

    pl.semaphore_wait(barrier, n_head - 1 + n_bits + 2)

    def spread(i, src, dst, first):
        copies = []
        for d in range(1, n_head):
            to = lax.rem(head + d, n_head)
            cols = pl.ds(pl.multiple_of(to * fw, fw), fw)
            rows = pl.ds(pl.multiple_of(first + head * tok, tok), tok)
            copies.append(
                pltpu.make_async_remote_copy(
                    src_ref=src.at[:, cols],
                    dst_ref=dst.at[rows, :],
                    send_sem=a2a_send.at[i, d - 1],
                    recv_sem=a2a_recv.at[i, d - 1],
                    device_id={"head": to},
                    device_id_type=MESH,
                )
            )
        return copies

    k_copies = spread(0, k_hbm, k_all, WIN)
    v_copies = spread(1, v_hbm, v_all, WIN)
    q_copies = spread(2, q_hbm, q_all, 0)
    for c in k_copies + v_copies:
        c.start()
    sent = k_copies + v_copies + q_copies

    for c in small:
        c.wait()
    for i in range(count // 128):
        wide = jnp.broadcast_to(step_ref[0:1, i * 128 : (i + 1) * 128], (128, 128))
        step_t[i * 128 : (i + 1) * 128, :] = wide.T

    init_copy.wait()
    for m in range(3):
        wb[m] = w32[m].astype(BF)

    def chunks(rows, body, size=64):
        def go(i, carry):
            body(pl.ds(pl.multiple_of(i * size, size), size), i * size)
            return carry

        lax.fori_loop(0, rows // size, go, 0)

    def rms(x):
        return x * lax.rsqrt(jnp.mean(x * x, axis=-1, keepdims=True) + 1e-06)

    def dot(a, b, ca=1, cb=0):
        return lax.dot_general(a, b, (((ca,), (cb,)), ((), ())), preferred_element_type=F32)

    def rms_keys(rows, first):
        kb[rows, :] = rms(k_all[pl.ds(pl.multiple_of(first + WIN, 64), 64), :].astype(F32)).astype(BF)

    def rms_queries(rows, first):
        qb[rows, :] = rms(q_all[rows, :].astype(F32)).astype(BF)

    def inside(first, size, block):
        pos = ctx * count + first + lax.broadcasted_iota(jnp.int32, (size, 128), 0)
        early = pos < bound_ref[0]
        return early if block == 0 else jnp.logical_not(early)

    def make_target(block):
        def body(rows, first):
            col = jnp.where(inside(first, 64, block), step_t[rows, :], 0.0)
            scale = jnp.concatenate([col] * (fw // 128), axis=1)
            v = v_all[pl.ds(pl.multiple_of(first + WIN, 64), 64), :].astype(F32)
            tgt[rows, :] = (v * scale).astype(BF)

        chunks(count, body)

    def make_hidden():
        def body(rows, first):
            g = pre[0, rows, :]
            u = pre[1, rows, :]
            act = g * jax.nn.sigmoid(g)
            hid[rows, :] = (act * u).astype(BF)

        chunks(count, body)

    def make_back(with_hidden):
        def body(rows, first):
            g = pre[0, rows, :]
            u = pre[1, rows, :]
            o = back[rows, :]
            sig = jax.nn.sigmoid(g)
            act = g * sig
            if with_hidden:
                hid[rows, :] = (act * u).astype(BF)
            bg[rows, :] = (o * u * sig * (1.0 + g * (1.0 - sig))).astype(BF)
            bu[rows, :] = (o * act).astype(BF)

        chunks(count, body)

    def ctx_copy(block, m, src, dst, t, bit):
        c = pltpu.make_async_remote_copy(
            src_ref=src,
            dst_ref=dst,
            send_sem=ar_send.at[block, m, t],
            recv_sem=ar_recv.at[block, m, t],
            device_id={"ctx": partner(bit)},
            device_id_type=MESH,
        )
        c.start()
        sent.append(c)
        return c

    def al(x, n):
        return pl.multiple_of(x, n)

    def sum_steps(block, m):
        mine = bit_of(0) * half
        other = half - mine
        state = {}

        def first():
            sb[block, m, 0:half, :] = grad[m, pl.ds(al(other, half), half), :].astype(BF)
            state["c"] = [
                ctx_copy(block, m, sb.at[block, m, pl.ds(0, half)], rb.at[block, m, pl.ds(0, half)], 0, 0)
            ]
            state["base"] = [mine, mine + quarter]

        def land_first():
            state["c"][0].wait_recv()
            rows = pl.ds(al(mine, half), half)
            grad[m, rows, :] = grad[m, rows, :] + rb[block, m, 0:half, :].astype(F32)

        def launch(s):
            state["c"] = []
            for g, (steps, _) in enumerate(groups):
                bit, halve, size, part, off, t = steps[s]
                base = state["base"][g]
                if halve:
                    src = base + (1 - bit_of(bit)) * part
                    state["base"][g] = base + bit_of(bit) * part
                else:
                    src = base
                sb[block, m, off : off + part, :] = grad[m, pl.ds(al(src, part), part), :].astype(BF)
                area = pl.ds(off, part)
                state["c"].append(
                    ctx_copy(block, m, sb.at[block, m, area], rb.at[block, m, area], t, bit)
                )

        def land(s):
            for g, (steps, _) in enumerate(groups):
                bit, halve, size, part, off, t = steps[s]
                state["c"][g].wait_recv()
                rows = pl.ds(al(state["base"][g], part), part)
                grad[m, rows, :] = grad[m, rows, :] + rb[block, m, off : off + part, :].astype(F32)

        def settle():
            for g, (_, size) in enumerate(groups):
                rows = pl.ds(al(state["base"][g], size), size)
                red[block, m, rows, :] = grad[m, rows, :].astype(BF)

        n_steps = n_bits - 1

        def return_launch(s):
            state["c"] = []
            for g, (steps, _) in enumerate(groups):
                bit, halve, size, part, off, t = steps[s]
                if not halve:
                    continue
                rows = pl.ds(al(state["base"][g], part), part)
                here = red.at[block, m, rows]
                state["c"].append(
                    ctx_copy(block, m, here, here, back_at + g * n_steps + s, bit)
                )

        def return_land(s):
            for c in state["c"]:
                c.wait_recv()
            for g, (steps, _) in enumerate(groups):
                bit, halve, size, part, off, t = steps[s]
                if halve:
                    state["base"][g] = state["base"][g] - bit_of(bit) * part

        def last_launch():
            here = red.at[block, m, pl.ds(al(mine, half), half)]
            state["c"] = [ctx_copy(block, m, here, here, back_at + 2 * n_steps, 0)]

        def joint_launch():
            theirs = 1 - bit_of(0)
            here = red.at[block, theirs, pl.ds(al(mine, half), half)]
            state["c"] = [ctx_copy(block, m, here, here, back_at + 2 * n_steps, 0)]

        def last_land():
            state["c"][0].wait_recv()

        acts = [first, land_first]
        for s in range(n_steps):
            acts += [functools.partial(launch, s), functools.partial(land, s)]
        acts.append(settle)
        for s in reversed(range(n_steps)):
            acts += [functools.partial(return_launch, s), functools.partial(return_land, s)]
        if m == 2:
            acts += [last_launch, last_land]
        elif m == 1:
            acts += [joint_launch, last_land]
        steps, now = [], []
        for a in acts:
            name = a.func if isinstance(a, functools.partial) else a
            now.append(a)
            if name in (first, launch, return_launch, last_launch, joint_launch):
                steps.append(now)
                now = []
        steps.append(now)
        return steps

    def newton_schulz(block, m, out):
        r = red[block, m].astype(F32)
        inv = 1.0 / (jnp.sqrt(jnp.sum(r * r, keepdims=True)) + 1e-07)
        xs[...] = (r * inv).astype(BF)
        for step in range(NS_STEPS):
            sq[...] = dot(xs[...], xs[...], 1, 1).astype(BF)
            mx[...] = (ns_cubic * sq[...].astype(F32) + ns_quintic * dot(sq[...], sq[...])).astype(BF)
            x = (ns_linear * xs[...].astype(F32) + dot(mx[...], xs[...])).astype(BF)
            if step < NS_STEPS - 1:
                xs[...] = x
            else:
                out[...] = x

    def add_update(m, x):
        new = w32[m] + x[...].astype(F32)
        w32[m] = new
        wb[m] = new.astype(BF)

    def down_update(block):
        newton_schulz(block, 2, xs)
        add_update(2, xs)

    def pair_update(block, rows_in):
        own = bit_of(0)
        newton_schulz(block, own, x_out.at[block])
        c = pltpu.make_async_remote_copy(
            src_ref=x_out.at[block],
            dst_ref=x_in.at[block],
            send_sem=x_send.at[block],
            recv_sem=x_recv.at[block],
            device_id={"ctx": partner(0)},
            device_id_type=MESH,
        )
        c.start()
        sent.append(c)
        add_update(own, x_out.at[block])
        pre[own] = dot(rows_in[...], wb[own])
        c.wait_recv()
        add_update(1 - own, x_in.at[block])
        pre[1 - own] = dot(rows_in[...], wb[1 - own])

    ORDER = (2, 0, 1)

    def run_sums(block, before, after, fillers):
        todo, n_steps = [], 0
        for i, m in enumerate(ORDER):
            for s, acts in enumerate(sum_steps(block, m)):
                todo.append((s + LAG * min(i, 1) if s > 0 else 0, i, s, m, acts))
                n_steps = max(s, n_steps)
        fillers = list(fillers)
        for level in range(n_steps + LAG + 1):
            work = []
            for at, i, s, m, acts in todo:
                if at != level:
                    continue
                if s == 0:
                    before[m]()
                for a in acts:
                    a()
                if s == n_steps and m in after:
                    work.append(after[m])
            if level > 0 and fillers:
                fillers.pop(0)()
            for w in work:
                w()
        for f in fillers:
            f()

    def attend(j):
        cols = slice(j * AH, (j + 1) * AH)
        reach = win_ref[head * (fw // AH) + j]
        for i in range(count // WIN):
            q = q_all[i * WIN : (i + 1) * WIN, cols]
            keys = k_all[i * WIN : (i + 2) * WIN, cols]
            vals = v_all[i * WIN : (i + 2) * WIN, cols]
            scores = dot(q, keys, 1, 1) * (1.0 / math.sqrt(AH))
            row = lax.broadcasted_iota(jnp.int32, (WIN, 2 * WIN), 0)
            col = lax.broadcasted_iota(jnp.int32, (WIN, 2 * WIN), 1)
            gap = row + WIN - col
            allowed = (gap >= 0) & (gap < reach)
            if i == 0:
                allowed = allowed & (ctx * count - WIN + col >= 0)
            masked = jnp.where(allowed, scores, -jnp.inf)
            e = jnp.exp(masked - jnp.max(masked, axis=-1, keepdims=True))
            w = (e * (1.0 / jnp.sum(e, axis=-1, keepdims=True))).astype(BF)
            attended[i * WIN : (i + 1) * WIN, cols] = dot(w, vals).astype(BF)

    for c in locals_[:1]:
        c.wait()
    for c in k_copies:
        c.wait_recv()
    chunks(count, rms_keys)
    kbt[...] = kb[...].T
    pre[0] = dot(kb[...], wb[0])
    pre[1] = dot(kb[...], wb[1])
    make_hidden()
    locals_[1].wait()
    for c in v_copies:
        c.wait_recv()
    for c in q_copies:
        c.start()
    halos = []
    for i, ref in enumerate((k_all, v_all)):
        halos.append(
            pltpu.make_async_remote_copy(
                src_ref=ref.at[pl.ds(count, WIN)],
                dst_ref=ref.at[pl.ds(0, WIN)],
                send_sem=halo_send.at[i],
                recv_sem=halo_recv.at[i],
                device_id={"ctx": nxt},
                device_id_type=MESH,
            )
        )
    sent.extend(halos)

    def grad_down():
        grad[2] = dot(hid[...], tgt[...], 0, 0)

    def grad_gate():
        grad[0] = dot(kbt[...], bg[...])

    def grad_up():
        grad[1] = dot(kbt[...], bu[...])

    def first_gate():
        back[...] = dot(tgt[...], wb[2], 1, 1)
        make_back(False)
        grad_gate()

    def mid_down():
        down_update(0)
        make_target(1)
        back[...] = dot(tgt[...], wb[2], 1, 1)

    def mid_pair():
        for c in halos:
            c.start()
        pair_update(0, kb)
        make_back(True)

    def end_down():
        down_update(1)

    def end_pair():
        pair_update(1, qb)

    def got_queries():
        locals_[2].wait()
        for c in q_copies:
            c.wait_recv()
        chunks(count, rms_queries)
        pre[0] = dot(qb[...], wb[0])
        pre[1] = dot(qb[...], wb[1])

    def early_out():
        make_hidden()
        res1[...] = dot(hid[...], wb[2])

    def attend_first():
        for c in halos:
            c.wait_recv()
        attend(0)

    def finish_rows(rows, first):
        early = jnp.concatenate([inside(first, 64, 0)] * (fw // 128), axis=1)
        r = rms(jnp.where(early, res1[rows, :], back[rows, :]))
        out_ref[rows, :] = (attended[rows, :].astype(F32) + r).astype(BF)

    make_target(0)
    run_sums(0, {2: grad_down, 0: first_gate, 1: grad_up}, {2: mid_down, 1: mid_pair}, [])
    fill = [got_queries, early_out, attend_first]
    fill += [functools.partial(attend, j) for j in range(1, fw // AH)]
    run_sums(
        1, {2: grad_down, 0: grad_gate, 1: grad_up}, {2: end_down, 1: end_pair}, fill
    )
    make_hidden()
    back[...] = dot(hid[...], wb[2])
    chunks(count, finish_rows)
    for c in sent:
        c.wait_send()


def local(attn_q, attn_k, attn_v, step_size, fast_init, boundary, window_len):
    n_ctx = lax.axis_size("ctx")
    n_head = lax.axis_size("head")
    tok, width = attn_q.shape
    fw = width // n_head
    count = tok * n_head
    _, staged, _, transfers = sum_plan(fw, n_ctx.bit_length() - 1)
    hbm = pl.BlockSpec(memory_space=pltpu.HBM)
    vmem = pl.BlockSpec(memory_space=pltpu.VMEM)
    big = lambda dtype, *lead: pltpu.VMEM(lead + (count, fw), dtype)
    mat = lambda dtype, *lead: pltpu.VMEM(lead + (fw, fw), dtype)
    return pl.pallas_call(
        functools.partial(kernel, n_ctx, n_head),
        out_shape=jax.ShapeDtypeStruct((count, fw), BF),
        in_specs=[hbm] * 7,
        out_specs=vmem,
        scratch_shapes=[
            big(BF),
            pltpu.VMEM((count + WIN, fw), BF),
            pltpu.VMEM((count + WIN, fw), BF),
            big(BF),
            pltpu.VMEM((fw, count), BF),
            big(BF),
            pltpu.VMEM((count, 128), F32),
            mat(F32, 3),
            mat(BF, 3),
            big(F32, 2),
            big(F32),
            big(BF),
            big(BF),
            big(BF),
            big(BF),
            mat(BF),
            mat(BF),
            mat(BF),
            mat(F32, 3),
            big(BF),
            big(F32),
            pltpu.VMEM((2, 3, staged, fw), BF),
            pltpu.VMEM((2, 3, staged, fw), BF),
            mat(BF, 2, 3),
            mat(BF, 2),
            mat(BF, 2),
            pltpu.VMEM(step_size.shape, F32),
            pltpu.SMEM(boundary.shape, jnp.int32),
            pltpu.SMEM(window_len.shape, jnp.int32),
            pltpu.SemaphoreType.DMA((7,)),
            pltpu.SemaphoreType.DMA((3, n_head - 1)),
            pltpu.SemaphoreType.DMA((3, n_head - 1)),
            pltpu.SemaphoreType.DMA((2,)),
            pltpu.SemaphoreType.DMA((2,)),
            pltpu.SemaphoreType.DMA((2, 3, transfers)),
            pltpu.SemaphoreType.DMA((2, 3, transfers)),
            pltpu.SemaphoreType.DMA((2,)),
            pltpu.SemaphoreType.DMA((2,)),
        ],
        compiler_params=pltpu.CompilerParams(
            collective_id=0, has_side_effects=True, vmem_limit_bytes=60 * 1024 * 1024
        ),
    )(attn_q, attn_k, attn_v, step_size, fast_init, boundary, window_len)


def solution(mesh):
    return jax.shard_map(
        local,
        mesh=mesh,
        in_specs=(
            P(("ctx", "head"), None),
            P(("ctx", "head"), None),
            P(("ctx", "head"), None),
            P("head", "ctx"),
            P("head", None, None, None),
            P(),
            P(),
        ),
        out_specs=P("ctx", "head"),
        check_vma=False,
    )
```

```python
import functools
import math

import jax
import jax.numpy as jnp
from jax import lax
from jax.experimental import pallas as pl
from jax.experimental.pallas import tpu as pltpu
from jax.sharding import PartitionSpec as P

AH = 128
WIN = 128
NS_STEPS = 2
LAG = 1
ns_linear = 3.4445
ns_cubic = -4.775
ns_quintic = 2.0315
MESH = pl.DeviceIdType.MESH
F32 = jnp.float32
BF = jnp.bfloat16


def sum_plan(rows, n_bits):
    half = rows // 2
    quarter = half // 2
    offset = half
    transfers = 1
    groups = []
    for order in (list(range(1, n_bits)), list(range(n_bits - 1, 0, -1))):
        size = quarter
        steps = []
        for bit in order:
            halve = size // 2 >= 16
            sent = size // 2 if halve else size
            steps.append((bit, halve, size, sent, offset, transfers))
            offset += sent
            transfers += 1
            size = sent
        groups.append((steps, size))
    back = transfers
    transfers += 2 * (n_bits - 1) + 1
    return groups, offset, back, transfers


def kernel(
    n_ctx, n_head, q_hbm, k_hbm, v_hbm, step_hbm, init_hbm, bound_hbm, win_hbm, out_ref,
    q_all, k_all, v_all, kb, kbt, qb, step_t, w32, wb, pre, back, hid, tgt, bg, bu, xs, sq, mx,
    grad, attended, res1, sb, rb, red, x_out, x_in, step_ref, bound_ref, win_ref,
    loc_sem, a2a_send, a2a_recv, halo_send, halo_recv, ar_send, ar_recv, x_send, x_recv,
):
    ctx = lax.axis_index("ctx")
    head = lax.axis_index("head")
    n_bits = n_ctx.bit_length() - 1
    tok = q_hbm.shape[0]
    fw = q_all.shape[1]
    count = q_all.shape[0]
    half = fw // 2
    quarter = half // 2
    groups, _, back_at, _ = sum_plan(fw, n_bits)

    def bit_of(b):
        return lax.rem(lax.div(ctx, 1 << b), 2)

    def partner(b):
        return ctx + (1 << b) - 2 * (1 << b) * bit_of(b)

    nxt = lax.rem(ctx + 1, n_ctx)
    prv = lax.rem(ctx + n_ctx - 1, n_ctx)

    barrier = pltpu.get_barrier_semaphore()
    for d in range(1, n_head):
        pl.semaphore_signal(
            barrier, inc=1, device_id={"head": lax.rem(head + d, n_head)}, device_id_type=MESH
        )
    for b in range(n_bits):
        pl.semaphore_signal(barrier, inc=1, device_id={"ctx": partner(b)}, device_id_type=MESH)
    pl.semaphore_signal(barrier, inc=1, device_id={"ctx": nxt}, device_id_type=MESH)
    pl.semaphore_signal(barrier, inc=1, device_id={"ctx": prv}, device_id_type=MESH)

    my_cols = pl.ds(pl.multiple_of(head * fw, fw), fw)

    def own_copy(i, src, dst, first):
        rows = pl.ds(pl.multiple_of(first + head * tok, tok), tok)
        return pltpu.make_async_copy(src.at[:, my_cols], dst.at[rows, :], loc_sem.at[i])

    locals_ = [own_copy(0, k_hbm, k_all, WIN), own_copy(1, v_hbm, v_all, WIN), own_copy(2, q_hbm, q_all, 0)]
    init_copy = pltpu.make_async_copy(init_hbm.at[0], w32, loc_sem.at[3])
    for c in locals_:
        c.start()
    init_copy.start()
    small = [
        pltpu.make_async_copy(src, dst, loc_sem.at[4 + i])
        for i, (src, dst) in enumerate(
            ((step_hbm, step_ref), (bound_hbm, bound_ref), (win_hbm, win_ref))
        )
    ]
    for c in small:
        c.start()

    pl.semaphore_wait(barrier, n_head - 1 + n_bits + 2)

    def spread(i, src, dst, first):
        copies = []
        for d in range(1, n_head):
            to = lax.rem(head + d, n_head)
            cols = pl.ds(pl.multiple_of(to * fw, fw), fw)
            rows = pl.ds(pl.multiple_of(first + head * tok, tok), tok)
            copies.append(
                pltpu.make_async_remote_copy(
                    src_ref=src.at[:, cols],
                    dst_ref=dst.at[rows, :],
                    send_sem=a2a_send.at[i, d - 1],
                    recv_sem=a2a_recv.at[i, d - 1],
                    device_id={"head": to},
                    device_id_type=MESH,
                )
            )
        return copies

    k_copies = spread(0, k_hbm, k_all, WIN)
    v_copies = spread(1, v_hbm, v_all, WIN)
    q_copies = spread(2, q_hbm, q_all, 0)
    for c in k_copies + v_copies:
        c.start()
    sent = k_copies + v_copies + q_copies

    for c in small:
        c.wait()
    for i in range(count // 128):
        wide = jnp.broadcast_to(step_ref[0:1, i * 128 : (i + 1) * 128], (128, 128))
        step_t[i * 128 : (i + 1) * 128, :] = wide.T

    init_copy.wait()
    for m in range(3):
        wb[m] = w32[m].astype(BF)

    def chunks(rows, body, size=64):
        def go(i, carry):
            body(pl.ds(pl.multiple_of(i * size, size), size), i * size)
            return carry

        lax.fori_loop(0, rows // size, go, 0)

    def rms(x):
        return x * lax.rsqrt(jnp.mean(x * x, axis=-1, keepdims=True) + 1e-06)

    def dot(a, b, ca=1, cb=0):
        return lax.dot_general(a, b, (((ca,), (cb,)), ((), ())), preferred_element_type=F32)

    def rms_keys(rows, first):
        kb[rows, :] = rms(k_all[pl.ds(pl.multiple_of(first + WIN, 64), 64), :].astype(F32)).astype(BF)

    def rms_queries(rows, first):
        qb[rows, :] = rms(q_all[rows, :].astype(F32)).astype(BF)

    def inside(first, size, block):
        pos = ctx * count + first + lax.broadcasted_iota(jnp.int32, (size, 128), 0)
        early = pos < bound_ref[0]
        return early if block == 0 else jnp.logical_not(early)

    def make_target(block):
        def body(rows, first):
            col = jnp.where(inside(first, 64, block), step_t[rows, :], 0.0)
            scale = jnp.concatenate([col] * (fw // 128), axis=1)
            v = v_all[pl.ds(pl.multiple_of(first + WIN, 64), 64), :].astype(F32)
            tgt[rows, :] = (v * scale).astype(BF)

        chunks(count, body)

    def sigmoid(x):
        return 0.5 * jnp.tanh(0.5 * x) + 0.5

    def make_hidden():
        def body(rows, first):
            g = pre[0, rows, :]
            u = pre[1, rows, :]
            act = g * sigmoid(g)
            hid[rows, :] = (act * u).astype(BF)

        chunks(count, body)

    def make_back(with_hidden):
        def body(rows, first):
            g = pre[0, rows, :]
            u = pre[1, rows, :]
            o = back[rows, :]
            sig = sigmoid(g)
            act = g * sig
            if with_hidden:
                hid[rows, :] = (act * u).astype(BF)
            bg[rows, :] = (o * u * sig * (1.0 + g * (1.0 - sig))).astype(BF)
            bu[rows, :] = (o * act).astype(BF)

        chunks(count, body)

    def ctx_copy(block, m, src, dst, t, bit):
        c = pltpu.make_async_remote_copy(
            src_ref=src,
            dst_ref=dst,
            send_sem=ar_send.at[block, m, t],
            recv_sem=ar_recv.at[block, m, t],
            device_id={"ctx": partner(bit)},
            device_id_type=MESH,
        )
        c.start()
        sent.append(c)
        return c

    def al(x, n):
        return pl.multiple_of(x, n)

    def sum_steps(block, m):
        mine = bit_of(0) * half
        other = half - mine
        state = {}

        def first():
            sb[block, m, 0:half, :] = grad[m, pl.ds(al(other, half), half), :].astype(BF)
            state["c"] = [
                ctx_copy(block, m, sb.at[block, m, pl.ds(0, half)], rb.at[block, m, pl.ds(0, half)], 0, 0)
            ]
            state["base"] = [mine, mine + quarter]

        def land_first():
            state["c"][0].wait_recv()
            rows = pl.ds(al(mine, half), half)
            grad[m, rows, :] = grad[m, rows, :] + rb[block, m, 0:half, :].astype(F32)

        def launch(s):
            state["c"] = []
            for g, (steps, _) in enumerate(groups):
                bit, halve, size, part, off, t = steps[s]
                base = state["base"][g]
                if halve:
                    src = base + (1 - bit_of(bit)) * part
                    state["base"][g] = base + bit_of(bit) * part
                else:
                    src = base
                sb[block, m, off : off + part, :] = grad[m, pl.ds(al(src, part), part), :].astype(BF)
                area = pl.ds(off, part)
                state["c"].append(
                    ctx_copy(block, m, sb.at[block, m, area], rb.at[block, m, area], t, bit)
                )

        def land(s):
            for g, (steps, _) in enumerate(groups):
                bit, halve, size, part, off, t = steps[s]
                state["c"][g].wait_recv()
                rows = pl.ds(al(state["base"][g], part), part)
                grad[m, rows, :] = grad[m, rows, :] + rb[block, m, off : off + part, :].astype(F32)

        def settle():
            for g, (_, size) in enumerate(groups):
                rows = pl.ds(al(state["base"][g], size), size)
                red[block, m, rows, :] = grad[m, rows, :].astype(BF)

        n_steps = n_bits - 1

        def return_launch(s):
            state["c"] = []
            for g, (steps, _) in enumerate(groups):
                bit, halve, size, part, off, t = steps[s]
                if not halve:
                    continue
                rows = pl.ds(al(state["base"][g], part), part)
                here = red.at[block, m, rows]
                state["c"].append(
                    ctx_copy(block, m, here, here, back_at + g * n_steps + s, bit)
                )

        def return_land(s):
            for c in state["c"]:
                c.wait_recv()
            for g, (steps, _) in enumerate(groups):
                bit, halve, size, part, off, t = steps[s]
                if halve:
                    state["base"][g] = state["base"][g] - bit_of(bit) * part

        def last_launch():
            here = red.at[block, m, pl.ds(al(mine, half), half)]
            state["c"] = [ctx_copy(block, m, here, here, back_at + 2 * n_steps, 0)]

        def joint_launch():
            theirs = 1 - bit_of(0)
            here = red.at[block, theirs, pl.ds(al(mine, half), half)]
            state["c"] = [ctx_copy(block, m, here, here, back_at + 2 * n_steps, 0)]

        def last_land():
            state["c"][0].wait_recv()

        acts = [first, land_first]
        for s in range(n_steps):
            acts += [functools.partial(launch, s), functools.partial(land, s)]
        acts.append(settle)
        for s in reversed(range(n_steps)):
            acts += [functools.partial(return_launch, s), functools.partial(return_land, s)]
        if m == 2:
            acts += [last_launch, last_land]
        elif m == 1:
            acts += [joint_launch, last_land]
        steps, now = [], []
        for a in acts:
            name = a.func if isinstance(a, functools.partial) else a
            now.append(a)
            if name in (first, launch, return_launch, last_launch, joint_launch):
                steps.append(now)
                now = []
        steps.append(now)
        return steps

    def ns_step(out, rows_done=None):
        sq[...] = dot(xs[...], xs[...], 1, 1).astype(BF)
        mx[...] = (ns_cubic * sq[...].astype(F32) + ns_quintic * dot(sq[...], sq[...])).astype(BF)
        if rows_done is None:
            out[...] = (ns_linear * xs[...].astype(F32) + dot(mx[...], xs[...])).astype(BF)
        else:
            for i in range(2):
                rows = slice(i * half, (i + 1) * half)
                out[rows, :] = (
                    ns_linear * xs[rows, :].astype(F32) + dot(mx[rows, :], xs[...])
                ).astype(BF)
                rows_done(i)

    def ns_start(block, m):
        r = red[block, m].astype(F32)
        inv = 1.0 / (jnp.sqrt(jnp.sum(r * r, keepdims=True)) + 1e-07)
        xs[...] = (r * inv).astype(BF)
        for _ in range(NS_STEPS - 1):
            ns_step(xs)

    def add_update(m, x):
        new = w32[m] + x[...].astype(F32)
        w32[m] = new
        wb[m] = new.astype(BF)

    def down_update():
        ns_step(xs)
        add_update(2, xs)

    def pair_update(block, rows_in):
        own = bit_of(0)
        copies = []

        def rows_done(i):
            c = pltpu.make_async_remote_copy(
                src_ref=x_out.at[block, pl.ds(i * half, half)],
                dst_ref=x_in.at[block, pl.ds(i * half, half)],
                send_sem=x_send.at[block, i],
                recv_sem=x_recv.at[block, i],
                device_id={"ctx": partner(0)},
                device_id_type=MESH,
            )
            c.start()
            copies.append(c)

        ns_start(block, own)
        ns_step(x_out.at[block], rows_done)
        sent.extend(copies)
        add_update(own, x_out.at[block])
        pre[own] = dot(rows_in[...], wb[own])
        for c in copies:
            c.wait_recv()
        add_update(1 - own, x_in.at[block])
        pre[1 - own] = dot(rows_in[...], wb[1 - own])

    ORDER = (2, 0, 1)

    def run_sums(block, before, after, fillers):
        todo, n_steps = [], 0
        for i, m in enumerate(ORDER):
            for s, acts in enumerate(sum_steps(block, m)):
                todo.append((s + LAG * min(i, 1) if s > 0 else 0, i, s, m, acts))
                n_steps = max(s, n_steps)
        fillers = list(fillers)
        for level in range(n_steps + LAG + 1):
            work = []
            for at, i, s, m, acts in todo:
                if at != level:
                    continue
                if s == 0:
                    before[m]()
                for a in acts:
                    a()
                if s == n_steps and m in after:
                    if m == 2:
                        ns_start(block, m)
                    work.append(after[m])
            if level > 0 and fillers:
                fillers.pop(0)()
            for w in work:
                w()
        for f in fillers:
            f()

    def attend(j):
        cols = slice(j * AH, (j + 1) * AH)
        reach = win_ref[head * (fw // AH) + j]
        for i in range(count // WIN):
            q = q_all[i * WIN : (i + 1) * WIN, cols]
            keys = k_all[i * WIN : (i + 2) * WIN, cols]
            vals = v_all[i * WIN : (i + 2) * WIN, cols]
            scores = dot(q, keys, 1, 1) * (1.0 / math.sqrt(AH))
            row = lax.broadcasted_iota(jnp.int32, (WIN, 2 * WIN), 0)
            col = lax.broadcasted_iota(jnp.int32, (WIN, 2 * WIN), 1)
            gap = row + WIN - col
            allowed = (gap >= 0) & (gap < reach)
            if i == 0:
                allowed = allowed & (ctx * count - WIN + col >= 0)
            masked = jnp.where(allowed, scores, -jnp.inf)
            e = jnp.exp(masked - jnp.max(masked, axis=-1, keepdims=True))
            w = (e * (1.0 / jnp.sum(e, axis=-1, keepdims=True))).astype(BF)
            attended[i * WIN : (i + 1) * WIN, cols] = dot(w, vals).astype(BF)

    for c in locals_[:1]:
        c.wait()
    for c in k_copies:
        c.wait_recv()
    chunks(count, rms_keys)
    kbt[...] = kb[...].T
    pre[0] = dot(kb[...], wb[0])
    pre[1] = dot(kb[...], wb[1])
    make_hidden()
    locals_[1].wait()
    for c in v_copies:
        c.wait_recv()
    for c in q_copies:
        c.start()
    halos = []
    for i, ref in enumerate((k_all, v_all)):
        halos.append(
            pltpu.make_async_remote_copy(
                src_ref=ref.at[pl.ds(count, WIN)],
                dst_ref=ref.at[pl.ds(0, WIN)],
                send_sem=halo_send.at[i],
                recv_sem=halo_recv.at[i],
                device_id={"ctx": nxt},
                device_id_type=MESH,
            )
        )
    sent.extend(halos)

    def grad_down():
        grad[2] = dot(hid[...], tgt[...], 0, 0)

    def grad_gate():
        grad[0] = dot(kbt[...], bg[...])

    def grad_up():
        grad[1] = dot(kbt[...], bu[...])

    def first_gate():
        back[...] = dot(tgt[...], wb[2], 1, 1)
        make_back(False)
        grad_gate()

    def mid_down():
        down_update()
        make_target(1)
        back[...] = dot(tgt[...], wb[2], 1, 1)

    def mid_pair():
        for c in halos:
            c.start()
        pair_update(0, kb)
        make_back(True)

    def end_down():
        down_update()

    def end_pair():
        pair_update(1, qb)

    def got_queries():
        locals_[2].wait()
        for c in q_copies:
            c.wait_recv()
        chunks(count, rms_queries)
        pre[0] = dot(qb[...], wb[0])
        pre[1] = dot(qb[...], wb[1])

    def early_out():
        make_hidden()
        res1[...] = dot(hid[...], wb[2])

    def attend_first():
        for c in halos:
            c.wait_recv()
        attend(0)

    def finish_rows(rows, first):
        early = jnp.concatenate([inside(first, 64, 0)] * (fw // 128), axis=1)
        r = rms(jnp.where(early, res1[rows, :], back[rows, :]))
        out_ref[rows, :] = (attended[rows, :].astype(F32) + r).astype(BF)

    make_target(0)
    run_sums(0, {2: grad_down, 0: first_gate, 1: grad_up}, {2: mid_down, 1: mid_pair}, [])
    fill = [got_queries, early_out, attend_first]
    fill += [functools.partial(attend, j) for j in range(1, fw // AH)]
    run_sums(
        1, {2: grad_down, 0: grad_gate, 1: grad_up}, {2: end_down, 1: end_pair}, fill
    )
    make_hidden()
    back[...] = dot(hid[...], wb[2])
    chunks(count, finish_rows)
    for c in sent:
        c.wait_send()


def local(attn_q, attn_k, attn_v, step_size, fast_init, boundary, window_len):
    n_ctx = lax.axis_size("ctx")
    n_head = lax.axis_size("head")
    tok, width = attn_q.shape
    fw = width // n_head
    count = tok * n_head
    _, staged, _, transfers = sum_plan(fw, n_ctx.bit_length() - 1)
    hbm = pl.BlockSpec(memory_space=pltpu.HBM)
    vmem = pl.BlockSpec(memory_space=pltpu.VMEM)
    big = lambda dtype, *lead: pltpu.VMEM(lead + (count, fw), dtype)
    mat = lambda dtype, *lead: pltpu.VMEM(lead + (fw, fw), dtype)
    return pl.pallas_call(
        functools.partial(kernel, n_ctx, n_head),
        out_shape=jax.ShapeDtypeStruct((count, fw), BF),
        in_specs=[hbm] * 7,
        out_specs=vmem,
        scratch_shapes=[
            big(BF),
            pltpu.VMEM((count + WIN, fw), BF),
            pltpu.VMEM((count + WIN, fw), BF),
            big(BF),
            pltpu.VMEM((fw, count), BF),
            big(BF),
            pltpu.VMEM((count, 128), F32),
            mat(F32, 3),
            mat(BF, 3),
            big(F32, 2),
            big(F32),
            big(BF),
            big(BF),
            big(BF),
            big(BF),
            mat(BF),
            mat(BF),
            mat(BF),
            mat(F32, 3),
            big(BF),
            big(F32),
            pltpu.VMEM((2, 3, staged, fw), BF),
            pltpu.VMEM((2, 3, staged, fw), BF),
            mat(BF, 2, 3),
            mat(BF, 2),
            mat(BF, 2),
            pltpu.VMEM(step_size.shape, F32),
            pltpu.SMEM(boundary.shape, jnp.int32),
            pltpu.SMEM(window_len.shape, jnp.int32),
            pltpu.SemaphoreType.DMA((7,)),
            pltpu.SemaphoreType.DMA((3, n_head - 1)),
            pltpu.SemaphoreType.DMA((3, n_head - 1)),
            pltpu.SemaphoreType.DMA((2,)),
            pltpu.SemaphoreType.DMA((2,)),
            pltpu.SemaphoreType.DMA((2, 3, transfers)),
            pltpu.SemaphoreType.DMA((2, 3, transfers)),
            pltpu.SemaphoreType.DMA((2, 2)),
            pltpu.SemaphoreType.DMA((2, 2)),
        ],
        compiler_params=pltpu.CompilerParams(
            collective_id=0, has_side_effects=True, vmem_limit_bytes=60 * 1024 * 1024
        ),
    )(attn_q, attn_k, attn_v, step_size, fast_init, boundary, window_len)


def solution(mesh):
    return jax.shard_map(
        local,
        mesh=mesh,
        in_specs=(
            P(("ctx", "head"), None),
            P(("ctx", "head"), None),
            P(("ctx", "head"), None),
            P("head", "ctx"),
            P("head", None, None, None),
            P(),
            P(),
        ),
        out_specs=P("ctx", "head"),
        check_vma=False,
    )
```

```python
import functools
import math

import jax
import jax.numpy as jnp
from jax import lax
from jax.experimental import pallas as pl
from jax.experimental.pallas import tpu as pltpu
from jax.sharding import PartitionSpec as P

AH = 128
WIN = 128
NS_STEPS = 2
LAG = 1
ns_linear = 3.4445
ns_cubic = -4.775
ns_quintic = 2.0315
MESH = pl.DeviceIdType.MESH
F32 = jnp.float32
BF = jnp.bfloat16


def sum_plan(rows, n_bits):
    half = rows // 2
    quarter = half // 2
    offset = half
    transfers = 1
    groups = []
    for order in (list(range(1, n_bits)), list(range(n_bits - 1, 0, -1))):
        size = quarter
        steps = []
        for bit in order:
            halve = size // 2 >= 16
            sent = size // 2 if halve else size
            steps.append((bit, halve, size, sent, offset, transfers))
            offset += sent
            transfers += 1
            size = sent
        groups.append((steps, size))
    back = transfers
    transfers += 2 * (n_bits - 1) + 1
    return groups, offset, back, transfers


def kernel(
    n_ctx, n_head, q_hbm, k_hbm, v_hbm, step_hbm, init_hbm, bound_hbm, win_hbm, out_ref,
    q_all, k_all, v_all, kb, kbt, qb, step_t, w32, wb, pre, back, hid, tgt, bg, bu, xs, sq, mx,
    grad, attended, res1, sb, rb, red, x_out, x_in, step_ref, bound_ref, win_ref,
    loc_sem, a2a_send, a2a_recv, halo_send, halo_recv, ar_send, ar_recv, x_send, x_recv,
):
    ctx = lax.axis_index("ctx")
    head = lax.axis_index("head")
    n_bits = n_ctx.bit_length() - 1
    tok = q_hbm.shape[0]
    fw = q_all.shape[1]
    count = q_all.shape[0]
    half = fw // 2
    quarter = half // 2
    groups, _, back_at, _ = sum_plan(fw, n_bits)

    def bit_of(b):
        return lax.rem(lax.div(ctx, 1 << b), 2)

    def partner(b):
        return ctx + (1 << b) - 2 * (1 << b) * bit_of(b)

    nxt = lax.rem(ctx + 1, n_ctx)
    prv = lax.rem(ctx + n_ctx - 1, n_ctx)

    barrier = pltpu.get_barrier_semaphore()
    for d in range(1, n_head):
        pl.semaphore_signal(
            barrier, inc=1, device_id={"head": lax.rem(head + d, n_head)}, device_id_type=MESH
        )
    for b in range(n_bits):
        pl.semaphore_signal(barrier, inc=1, device_id={"ctx": partner(b)}, device_id_type=MESH)
    pl.semaphore_signal(barrier, inc=1, device_id={"ctx": nxt}, device_id_type=MESH)
    pl.semaphore_signal(barrier, inc=1, device_id={"ctx": prv}, device_id_type=MESH)

    my_cols = pl.ds(pl.multiple_of(head * fw, fw), fw)

    def own_copy(i, src, dst, first):
        rows = pl.ds(pl.multiple_of(first + head * tok, tok), tok)
        return pltpu.make_async_copy(src.at[:, my_cols], dst.at[rows, :], loc_sem.at[i])

    locals_ = [own_copy(0, k_hbm, k_all, WIN), own_copy(1, v_hbm, v_all, WIN), own_copy(2, q_hbm, q_all, 0)]
    init_copy = pltpu.make_async_copy(init_hbm.at[0], w32, loc_sem.at[3])
    for c in locals_:
        c.start()
    init_copy.start()
    small = [
        pltpu.make_async_copy(src, dst, loc_sem.at[4 + i])
        for i, (src, dst) in enumerate(
            ((step_hbm, step_ref), (bound_hbm, bound_ref), (win_hbm, win_ref))
        )
    ]
    for c in small:
        c.start()

    pl.semaphore_wait(barrier, n_head - 1 + n_bits + 2)

    def spread(i, src, dst, first):
        copies = []
        for d in range(1, n_head):
            to = lax.rem(head + d, n_head)
            cols = pl.ds(pl.multiple_of(to * fw, fw), fw)
            rows = pl.ds(pl.multiple_of(first + head * tok, tok), tok)
            copies.append(
                pltpu.make_async_remote_copy(
                    src_ref=src.at[:, cols],
                    dst_ref=dst.at[rows, :],
                    send_sem=a2a_send.at[i, d - 1],
                    recv_sem=a2a_recv.at[i, d - 1],
                    device_id={"head": to},
                    device_id_type=MESH,
                )
            )
        return copies

    k_copies = spread(0, k_hbm, k_all, WIN)
    v_copies = spread(1, v_hbm, v_all, WIN)
    q_copies = spread(2, q_hbm, q_all, 0)
    for c in k_copies + v_copies:
        c.start()
    sent = k_copies + v_copies + q_copies

    for c in small:
        c.wait()
    for i in range(count // 128):
        wide = jnp.broadcast_to(step_ref[0:1, i * 128 : (i + 1) * 128], (128, 128))
        step_t[i * 128 : (i + 1) * 128, :] = wide.T

    init_copy.wait()
    for m in range(3):
        wb[m] = w32[m].astype(BF)

    def chunks(rows, body, size=64):
        def go(i, carry):
            body(pl.ds(pl.multiple_of(i * size, size), size), i * size)
            return carry

        lax.fori_loop(0, rows // size, go, 0)

    def rms(x):
        return x * lax.rsqrt(jnp.mean(x * x, axis=-1, keepdims=True) + 1e-06)

    def dot(a, b, ca=1, cb=0):
        return lax.dot_general(a, b, (((ca,), (cb,)), ((), ())), preferred_element_type=F32)

    def rms_keys(rows, first):
        kb[rows, :] = rms(k_all[pl.ds(pl.multiple_of(first + WIN, 64), 64), :].astype(F32)).astype(BF)

    def rms_queries(rows, first):
        qb[rows, :] = rms(q_all[rows, :].astype(F32)).astype(BF)

    def inside(first, size, block):
        pos = ctx * count + first + lax.broadcasted_iota(jnp.int32, (size, 128), 0)
        early = pos < bound_ref[0]
        return early if block == 0 else jnp.logical_not(early)

    def make_target(block):
        def body(rows, first):
            col = jnp.where(inside(first, 64, block), step_t[rows, :], 0.0)
            scale = jnp.concatenate([col] * (fw // 128), axis=1)
            v = v_all[pl.ds(pl.multiple_of(first + WIN, 64), 64), :].astype(F32)
            tgt[rows, :] = (v * scale).astype(BF)

        chunks(count, body)

    def sigmoid(x):
        return 0.5 * jnp.tanh(0.5 * x) + 0.5

    def make_hidden():
        def body(rows, first):
            g = pre[0, rows, :]
            u = pre[1, rows, :]
            act = g * sigmoid(g)
            hid[rows, :] = (act * u).astype(BF)

        chunks(count, body)

    def make_back(with_hidden):
        def body(rows, first):
            g = pre[0, rows, :]
            u = pre[1, rows, :]
            o = back[rows, :]
            sig = sigmoid(g)
            act = g * sig
            if with_hidden:
                hid[rows, :] = (act * u).astype(BF)
            bg[rows, :] = (o * u * sig * (1.0 + g * (1.0 - sig))).astype(BF)
            bu[rows, :] = (o * act).astype(BF)

        chunks(count, body)

    def ctx_copy(block, m, src, dst, t, bit):
        c = pltpu.make_async_remote_copy(
            src_ref=src,
            dst_ref=dst,
            send_sem=ar_send.at[block, m, t],
            recv_sem=ar_recv.at[block, m, t],
            device_id={"ctx": partner(bit)},
            device_id_type=MESH,
        )
        c.start()
        sent.append(c)
        return c

    def al(x, n):
        return pl.multiple_of(x, n)

    def sum_steps(block, m):
        mine = bit_of(0) * half
        other = half - mine
        state = {}

        def first():
            sb[block, m, 0:half, :] = grad[m, pl.ds(al(other, half), half), :].astype(BF)
            state["c"] = [
                ctx_copy(block, m, sb.at[block, m, pl.ds(0, half)], rb.at[block, m, pl.ds(0, half)], 0, 0)
            ]
            state["base"] = [mine, mine + quarter]

        def land_first():
            state["c"][0].wait_recv()
            rows = pl.ds(al(mine, half), half)
            grad[m, rows, :] = grad[m, rows, :] + rb[block, m, 0:half, :].astype(F32)

        def launch(s):
            state["c"] = []
            for g, (steps, _) in enumerate(groups):
                bit, halve, size, part, off, t = steps[s]
                base = state["base"][g]
                if halve:
                    src = base + (1 - bit_of(bit)) * part
                    state["base"][g] = base + bit_of(bit) * part
                else:
                    src = base
                sb[block, m, off : off + part, :] = grad[m, pl.ds(al(src, part), part), :].astype(BF)
                area = pl.ds(off, part)
                state["c"].append(
                    ctx_copy(block, m, sb.at[block, m, area], rb.at[block, m, area], t, bit)
                )

        def land(s):
            for g, (steps, _) in enumerate(groups):
                bit, halve, size, part, off, t = steps[s]
                state["c"][g].wait_recv()
                rows = pl.ds(al(state["base"][g], part), part)
                grad[m, rows, :] = grad[m, rows, :] + rb[block, m, off : off + part, :].astype(F32)

        def settle():
            for g, (_, size) in enumerate(groups):
                rows = pl.ds(al(state["base"][g], size), size)
                red[block, m, rows, :] = grad[m, rows, :].astype(BF)

        n_steps = n_bits - 1

        def return_launch(s):
            state["c"] = []
            for g, (steps, _) in enumerate(groups):
                bit, halve, size, part, off, t = steps[s]
                if not halve:
                    continue
                rows = pl.ds(al(state["base"][g], part), part)
                here = red.at[block, m, rows]
                state["c"].append(
                    ctx_copy(block, m, here, here, back_at + g * n_steps + s, bit)
                )

        def return_land(s):
            for c in state["c"]:
                c.wait_recv()
            for g, (steps, _) in enumerate(groups):
                bit, halve, size, part, off, t = steps[s]
                if halve:
                    state["base"][g] = state["base"][g] - bit_of(bit) * part

        def last_launch():
            here = red.at[block, m, pl.ds(al(mine, half), half)]
            state["c"] = [ctx_copy(block, m, here, here, back_at + 2 * n_steps, 0)]

        def joint_launch():
            theirs = 1 - bit_of(0)
            here = red.at[block, theirs, pl.ds(al(mine, half), half)]
            state["c"] = [ctx_copy(block, m, here, here, back_at + 2 * n_steps, 0)]

        def last_land():
            state["c"][0].wait_recv()

        acts = [first, land_first]
        for s in range(n_steps):
            acts += [functools.partial(launch, s), functools.partial(land, s)]
        acts.append(settle)
        for s in reversed(range(n_steps)):
            acts += [functools.partial(return_launch, s), functools.partial(return_land, s)]
        if m == 2:
            acts += [last_launch, last_land]
        elif m == 1:
            acts += [joint_launch, last_land]
        steps, now = [], []
        for a in acts:
            name = a.func if isinstance(a, functools.partial) else a
            now.append(a)
            if name in (first, launch, return_launch, last_launch, joint_launch):
                steps.append(now)
                now = []
        steps.append(now)
        return steps

    def ns_step(out, rows_done=None):
        sq[...] = dot(xs[...], xs[...], 1, 1).astype(BF)
        mx[...] = (ns_cubic * sq[...].astype(F32) + ns_quintic * dot(sq[...], sq[...])).astype(BF)
        if rows_done is None:
            out[...] = (ns_linear * xs[...].astype(F32) + dot(mx[...], xs[...])).astype(BF)
        else:
            for i in range(2):
                rows = slice(i * half, (i + 1) * half)
                out[rows, :] = (
                    ns_linear * xs[rows, :].astype(F32) + dot(mx[rows, :], xs[...])
                ).astype(BF)
                rows_done(i)

    def ns_start(block, m):
        r = red[block, m].astype(F32)
        inv = 1.0 / (jnp.sqrt(jnp.sum(r * r, keepdims=True)) + 1e-07)
        xs[...] = (r * inv).astype(BF)
        for _ in range(NS_STEPS - 1):
            ns_step(xs)

    def add_update(m, x):
        new = w32[m] + x[...].astype(F32)
        w32[m] = new
        wb[m] = new.astype(BF)

    def down_update():
        ns_step(xs)
        add_update(2, xs)

    def pair_update(block, rows_in):
        own = bit_of(0)
        copies = []

        def rows_done(i):
            c = pltpu.make_async_remote_copy(
                src_ref=x_out.at[block, pl.ds(i * half, half)],
                dst_ref=x_in.at[block, pl.ds(i * half, half)],
                send_sem=x_send.at[block, i],
                recv_sem=x_recv.at[block, i],
                device_id={"ctx": partner(0)},
                device_id_type=MESH,
            )
            c.start()
            copies.append(c)

        ns_start(block, own)
        ns_step(x_out.at[block], rows_done)
        sent.extend(copies)
        add_update(own, x_out.at[block])
        pre[own] = dot(rows_in[...], wb[own])
        for c in copies:
            c.wait_recv()
        add_update(1 - own, x_in.at[block])
        pre[1 - own] = dot(rows_in[...], wb[1 - own])

    ORDER = (2, 0, 1)

    def run_sums(block, before, after, fillers):
        todo, n_steps = [], 0
        for i, m in enumerate(ORDER):
            for s, acts in enumerate(sum_steps(block, m)):
                todo.append((s + LAG * min(i, 1) if s > 0 else 0, i, s, m, acts))
                n_steps = max(s, n_steps)
        fillers = list(fillers)
        for level in range(n_steps + LAG + 1):
            work = []
            for at, i, s, m, acts in todo:
                if at != level:
                    continue
                if s == 0:
                    before[m]()
                for a in acts:
                    a()
                if s == n_steps and m in after:
                    if m == 2:
                        ns_start(block, m)
                    work.append(after[m])
            f = fillers.pop(0) if level > 0 and fillers else None
            if f is not None:
                f()
            for w in work:
                w()
        for f in fillers:
            f()

    def attend(j, blocks):
        cols = slice(j * AH, (j + 1) * AH)
        reach = win_ref[head * (fw // AH) + j]
        for i in blocks:
            q = q_all[i * WIN : (i + 1) * WIN, cols]
            keys = k_all[i * WIN : (i + 2) * WIN, cols]
            vals = v_all[i * WIN : (i + 2) * WIN, cols]
            scores = dot(q, keys, 1, 1) * (1.0 / math.sqrt(AH))
            row = lax.broadcasted_iota(jnp.int32, (WIN, 2 * WIN), 0)
            col = lax.broadcasted_iota(jnp.int32, (WIN, 2 * WIN), 1)
            gap = row + WIN - col
            allowed = (gap >= 0) & (gap < reach)
            if i == 0:
                allowed = allowed & (ctx * count - WIN + col >= 0)
            masked = jnp.where(allowed, scores, -jnp.inf)
            e = jnp.exp(masked - jnp.max(masked, axis=-1, keepdims=True))
            w = (e * (1.0 / jnp.sum(e, axis=-1, keepdims=True))).astype(BF)
            attended[i * WIN : (i + 1) * WIN, cols] = dot(w, vals).astype(BF)

    for c in locals_[:1]:
        c.wait()
    for c in k_copies:
        c.wait_recv()
    chunks(count, rms_keys)
    kbt[...] = kb[...].T
    pre[0] = dot(kb[...], wb[0])
    pre[1] = dot(kb[...], wb[1])
    make_hidden()
    locals_[1].wait()
    for c in v_copies:
        c.wait_recv()
    for c in q_copies:
        c.start()
    halos = []
    for i, ref in enumerate((k_all, v_all)):
        halos.append(
            pltpu.make_async_remote_copy(
                src_ref=ref.at[pl.ds(count, WIN)],
                dst_ref=ref.at[pl.ds(0, WIN)],
                send_sem=halo_send.at[i],
                recv_sem=halo_recv.at[i],
                device_id={"ctx": nxt},
                device_id_type=MESH,
            )
        )
    sent.extend(halos)

    def grad_down():
        grad[2] = dot(hid[...], tgt[...], 0, 0)

    def grad_gate():
        grad[0] = dot(kbt[...], bg[...])

    def grad_up():
        grad[1] = dot(kbt[...], bu[...])

    def first_gate():
        back[...] = dot(tgt[...], wb[2], 1, 1)
        make_back(False)
        grad_gate()

    def mid_down():
        down_update()
        back[...] = dot(tgt[...], wb[2], 1, 1)

    def mid_pair():
        for c in halos:
            c.start()
        pair_update(0, kb)
        make_back(True)

    def end_down():
        down_update()

    def end_pair():
        pair_update(1, qb)

    n_heads = fw // AH

    def inner_rows(heads):
        for j in heads:
            attend(j, range(1, count // WIN))

    def got_queries():
        locals_[2].wait()
        for c in q_copies:
            c.wait_recv()
        chunks(count, rms_queries)
        inner_rows(range(n_heads // 2))

    def early_pre():
        pre[0] = dot(qb[...], wb[0])
        pre[1] = dot(qb[...], wb[1])

    def early_out():
        make_hidden()
        res1[...] = dot(hid[...], wb[2])

    def attend_first():
        for c in halos:
            c.wait_recv()
        for j in range(n_heads):
            attend(j, range(1))

    def finish_rows(rows, first):
        early = jnp.concatenate([inside(first, 64, 0)] * (fw // 128), axis=1)
        r = rms(jnp.where(early, res1[rows, :], back[rows, :]))
        out_ref[rows, :] = (attended[rows, :].astype(F32) + r).astype(BF)

    make_target(0)
    fill = [
        functools.partial(make_target, 1),
        None,
        None,
        got_queries,
        functools.partial(inner_rows, range(n_heads // 2, n_heads)),
    ]
    run_sums(0, {2: grad_down, 0: first_gate, 1: grad_up}, {2: mid_down, 1: mid_pair}, fill)
    fill = [early_pre, early_out, attend_first]
    run_sums(
        1, {2: grad_down, 0: grad_gate, 1: grad_up}, {2: end_down, 1: end_pair}, fill
    )
    make_hidden()
    back[...] = dot(hid[...], wb[2])
    chunks(count, finish_rows)
    for c in sent:
        c.wait_send()


def local(attn_q, attn_k, attn_v, step_size, fast_init, boundary, window_len):
    n_ctx = lax.axis_size("ctx")
    n_head = lax.axis_size("head")
    tok, width = attn_q.shape
    fw = width // n_head
    count = tok * n_head
    _, staged, _, transfers = sum_plan(fw, n_ctx.bit_length() - 1)
    hbm = pl.BlockSpec(memory_space=pltpu.HBM)
    vmem = pl.BlockSpec(memory_space=pltpu.VMEM)
    big = lambda dtype, *lead: pltpu.VMEM(lead + (count, fw), dtype)
    mat = lambda dtype, *lead: pltpu.VMEM(lead + (fw, fw), dtype)
    return pl.pallas_call(
        functools.partial(kernel, n_ctx, n_head),
        out_shape=jax.ShapeDtypeStruct((count, fw), BF),
        in_specs=[hbm] * 7,
        out_specs=vmem,
        scratch_shapes=[
            big(BF),
            pltpu.VMEM((count + WIN, fw), BF),
            pltpu.VMEM((count + WIN, fw), BF),
            big(BF),
            pltpu.VMEM((fw, count), BF),
            big(BF),
            pltpu.VMEM((count, 128), F32),
            mat(F32, 3),
            mat(BF, 3),
            big(F32, 2),
            big(F32),
            big(BF),
            big(BF),
            big(BF),
            big(BF),
            mat(BF),
            mat(BF),
            mat(BF),
            mat(F32, 3),
            big(BF),
            big(F32),
            pltpu.VMEM((2, 3, staged, fw), BF),
            pltpu.VMEM((2, 3, staged, fw), BF),
            mat(BF, 2, 3),
            mat(BF, 2),
            mat(BF, 2),
            pltpu.VMEM(step_size.shape, F32),
            pltpu.SMEM(boundary.shape, jnp.int32),
            pltpu.SMEM(window_len.shape, jnp.int32),
            pltpu.SemaphoreType.DMA((7,)),
            pltpu.SemaphoreType.DMA((3, n_head - 1)),
            pltpu.SemaphoreType.DMA((3, n_head - 1)),
            pltpu.SemaphoreType.DMA((2,)),
            pltpu.SemaphoreType.DMA((2,)),
            pltpu.SemaphoreType.DMA((2, 3, transfers)),
            pltpu.SemaphoreType.DMA((2, 3, transfers)),
            pltpu.SemaphoreType.DMA((2, 2)),
            pltpu.SemaphoreType.DMA((2, 2)),
        ],
        compiler_params=pltpu.CompilerParams(
            collective_id=0, has_side_effects=True, vmem_limit_bytes=60 * 1024 * 1024
        ),
    )(attn_q, attn_k, attn_v, step_size, fast_init, boundary, window_len)


def solution(mesh):
    return jax.shard_map(
        local,
        mesh=mesh,
        in_specs=(
            P(("ctx", "head"), None),
            P(("ctx", "head"), None),
            P(("ctx", "head"), None),
            P("head", "ctx"),
            P("head", None, None, None),
            P(),
            P(),
        ),
        out_specs=P("ctx", "head"),
        check_vma=False,
    )
```
